512 devices in a mesh: tm: 128 (over x, z, core), space: 4 (over y).
Axes of the slice: x: 4, y: 4, z: 16, core: 2. Of those that a mesh axis runs over, the one named last changes fastest.
Arguments:
- forcing: float32 [2048, 64, 2048], P('tm', 'space'), may hold values from -4 to 4
- iterate: float32 [512, 64, 2048], P('tm', 'space'), may hold values from -6 to 6
- permeability: float32 [64, 2048], P('space'), may hold values from 0.5 to 1
Outputs:
- updated: float32 [512, 64, 2048], P('tm', 'space')
The draws below stay inside these ranges and needn't reach their ends.
All inputs are finite; a program needn't handle non-finite values.
Results may differ from the reference program's by a relative error of at most 0.00002.
Values sent between devices are 32-bit elements; how exact they have to be, the bound alone decides.
A program may use at most 64 MiB of HBM per device.

```python
import math
import jax
import jax.numpy as jnp

COLS = 2048
SWEEPS = 6
NROWS = 64
STEPS = 2048
CPOINTS = 512
KPOINTS = 128


def block_scale(rng, extent, cuts, least, top_value):
    def one(axis_at, parts):
        steps = jax.random.uniform(jax.random.fold_in(jax.random.fold_in(rng, 6), axis_at), (parts,), jnp.float32, least / len(cuts), top_value / len(cuts))
        return jnp.repeat(jnp.exp(steps), extent[axis_at] // parts).reshape((-1,) + (1,) * (len(extent) - axis_at - 1))

    factor_of = one(*cuts[0])
    for cut in cuts[1:]:
        factor_of = factor_of * one(*cut)
    return factor_of


def noise(own_key, extent, spread, most, cuts=(), held_as=jnp.bfloat16):
    array = spread * jax.random.normal(own_key, extent, jnp.float32)
    if cuts:
        array = array * block_scale(own_key, extent, cuts, -0.22, 0.18)
    return jnp.clip(array, -most, most).astype(held_as)


def setup_inputs(seed: int = 0) -> dict:
    seeds = jax.random.split(jax.random.key(seed), 4)
    return {
        "forcing": noise(seeds[0], (STEPS, NROWS, COLS), 0.5, 4.0, ((0, 128), (1, 4)), jnp.float32),
        "iterate": noise(seeds[1], (CPOINTS, NROWS, COLS), 1.0, 6.0, ((0, 128), (1, 4)), jnp.float32),
        "permeability": jnp.clip(jnp.exp(math.log(1.0) - 0.6931472 * jax.random.uniform(seeds[2], (NROWS, COLS), jnp.float32) ** block_scale(seeds[2], (NROWS, COLS), ((0, 4),), -0.2, 0.2)), 0.5, 1.0),
    }


step_scale = 0.06


def stepper(field, coeff, factor):
    padded = jnp.pad(field, [(0, 0)] * (field.ndim - 1) + [(1, 1)])
    kpad = jnp.pad(coeff, ((0, 0), (1, 1)))
    center = padded[..., 1:-1, 1:-1]
    kmid = kpad[1:-1, 1:-1]
    flux = jnp.zeros_like(center)
    for rshift, cshift in ((1, 0), (-1, 0), (0, 1), (0, -1)):
        knext = kpad[1 + rshift:kpad.shape[0] - 1 + rshift, 1 + cshift:kpad.shape[1] - 1 + cshift]
        vnext = padded[..., 1 + rshift:padded.shape[-2] - 1 + rshift, 1 + cshift:padded.shape[-1] - 1 + cshift]
        flux = flux + 0.5 * (kmid + knext) * (vnext - center)
    return center + factor * flux


def operate(field, kpad_rows, factor):
    padded = jnp.pad(field, [(0, 0)] * (field.ndim - 2) + [(1, 1), (0, 0)])
    return stepper(padded, kpad_rows, factor)


def shifted(field):
    return jnp.concatenate([jnp.zeros_like(field[:1]), field[:-1]], axis=0)


def reference(forcing, iterate, permeability):
    kpad_rows = jnp.pad(permeability, ((1, 1), (0, 0)))
    c_fine = step_scale
    c_mid = 4.0 * step_scale
    c_top = 4.0 * step_scale
    blocks = forcing.reshape(CPOINTS, 4, NROWS, COLS)
    state = iterate
    for section in range(1, 4):
        state = operate(state, kpad_rows, c_fine) + blocks[:, section]
    ahead = operate(state, kpad_rows, c_fine)
    resid = (blocks[:, 0] + shifted(ahead)) - iterate
    rblocks = resid.reshape(KPOINTS, 4, NROWS, COLS)
    level = rblocks[:, 1]
    level = operate(level, kpad_rows, c_mid) + rblocks[:, 2]
    level = operate(level, kpad_rows, c_mid) + rblocks[:, 3]
    onward = operate(level, kpad_rows, c_mid)
    coarse_src = rblocks[:, 0] + shifted(onward)
    coarse = coarse_src
    for sweep in range(SWEEPS):
        coarse = coarse_src + operate(shifted(coarse), kpad_rows, c_top)
    first = operate(coarse, kpad_rows, c_mid) + rblocks[:, 1]
    second = operate(first, kpad_rows, c_mid) + rblocks[:, 2]
    third = operate(second, kpad_rows, c_mid) + rblocks[:, 3]
    correction = jnp.stack([coarse, first, second, third], axis=1).reshape(CPOINTS, NROWS, COLS)
    return iterate + correction
```

```python
import jax
import jax.numpy as jnp
from jax import lax
from jax.experimental import pallas as pl
from jax.experimental.pallas import tpu as pltpu
from jax.sharding import PartitionSpec as P

STEP = 0.06
NT = 128
NS = 4
ROWS = 16
EXT = 24
COLS = 2048
WIDTH = 512
MESH = pl.DeviceIdType.MESH
NCOPY = 112


def strips(body):
    def one(j, carry):
        body(pl.multiple_of(j * WIDTH, 128))
        return carry

    lax.fori_loop(0, COLS // WIDTH, one, 0)


def stencil(load, weights, at, rows):
    v = load(at, WIDTH)
    left = load(pl.multiple_of(lax.rem(at + COLS - 128, COLS), 128), 128)
    right = load(pl.multiple_of(lax.rem(at + WIDTH, COLS), 128), 128)
    wide = WIDTH + 128
    vl = pltpu.roll(jnp.concatenate([left[:rows], v[:rows]], axis=1), 1, axis=1)[:, 128:]
    vr = pltpu.roll(jnp.concatenate([v[:rows], right[:rows]], axis=1), wide - 1, axis=1)[:, :WIDTH]
    above = pltpu.roll(v, 1, axis=0)[:rows]
    below = pltpu.roll(v, EXT - 1, axis=0)[:rows]

    def w(i):
        return weights[i, 0:rows, pl.ds(at, WIDTH)]

    return w(0) * v[:rows] + w(1) * above + w(2) * below + (w(3) * vl + w(4) * vr)


def plain(ref, rows=EXT):
    return lambda at, width: ref[0:rows, pl.ds(at, width)]


def kernel(
    forcing, iterate, perm, out,
    f_buf, i_buf, k_buf, w_fine, w_mid, a_buf, ahead, r_buf, b_buf, g_buf, pg, ppg, ge_in,
    u_buf, u_in, y_buf, yc, m1, m1_in, q_buf, tmp, m2, m2_in, x_buf, e_buf, base, o_buf,
    send, recv, local, out_sem,
):
    t = lax.axis_index("tm")
    s = lax.axis_index("space")
    core = lax.rem(t, 2)
    chip = t // 2
    up = lax.rem(s + NS - 1, NS)
    down = lax.rem(s + 1, NS)
    mate = t + 1 - 2 * core
    count = [0]

    def shift(by):
        return lax.rem(t + by + NT, NT)

    def remote(src, dst, tm, sp):
        i = count[0]
        count[0] += 1
        return pltpu.make_async_remote_copy(
            src_ref=src, dst_ref=dst, send_sem=send.at[i], recv_sem=recv.at[i],
            device_id=(tm, sp), device_id_type=MESH,
        )

    def edges(src, dst, tm, depth):
        return [
            remote(src.at[0:depth], dst.at[ROWS : ROWS + depth], tm, up),
            remote(src.at[ROWS - depth : ROWS], dst.at[EXT - depth : EXT], tm, down),
        ]

    def start(copies):
        for c in copies:
            c.start()

    def arrive(copies):
        for c in copies:
            c.wait_recv()

    def sent(copies):
        for c in copies:
            c.wait_send()

    loads = [pltpu.make_async_copy(perm, k_buf.at[0:ROWS], local.at[0])]
    for p in range(4):
        loads.append(pltpu.make_async_copy(iterate.at[p], i_buf.at[p, 0:ROWS], local.at[1 + p]))
        loads.append(
            pltpu.make_async_copy(
                forcing.at[4 * p : 4 * p + 4], f_buf.at[4 * p : 4 * p + 4, 0:ROWS], local.at[5 + p]
            )
        )
    for c in loads:
        c.start()

    barrier = pltpu.get_barrier_semaphore()

    def greet(tm, sp):
        pl.semaphore_signal(barrier, inc=1, device_id=(tm, sp), device_id_type=MESH)

    greet(t, up)
    greet(t, down)
    greet(mate, s)
    for by in (-2, -4):
        for sp in (s, up, down):
            greet(shift(by), sp)

    @pl.when(core == 0)
    def _():
        for sp in (s, up, down):
            greet(shift(-3), sp)

    @pl.when(core == 1)
    def _():
        greet(shift(-3), s)
        for sp in (up, down):
            greet(mate, sp)

    pl.semaphore_wait(barrier, 12)

    k_halo = edges(perm, k_buf, t, 4)
    start(k_halo)
    halo = []
    for p in range(4):
        one = edges(iterate.at[p], i_buf.at[p], t, 4)
        for j in (1, 2, 3):
            one += edges(forcing.at[4 * p + j], f_buf.at[4 * p + j], t, 4 - j)
        if p == 0:
            one += edges(forcing.at[0], f_buf.at[0], t, 3)
        start(one)
        halo.append(one)

    for c in loads:
        c.wait()
    arrive(k_halo)

    row = lax.broadcasted_iota(jnp.int32, (EXT, 128), 0)
    is_below = jnp.logical_and(row >= ROWS, row < ROWS + 4)
    is_above = row >= ROWS + 4
    outside = jnp.logical_or(
        jnp.logical_and(is_below, s == NS - 1), jnp.logical_and(is_above, s == 0)
    )
    inside = jnp.where(outside, 0.0, 1.0).astype(jnp.float32)
    lane = lax.broadcasted_iota(jnp.int32, (EXT, 128), 1)

    def weigh(j, carry):
        at = pl.multiple_of(j * 128, 128)
        last = COLS // 128 - 1
        k = k_buf[:, pl.ds(at, 128)] * inside
        kl = k_buf[:, pl.ds(pl.multiple_of(lax.rem(at + COLS - 128, COLS), 128), 128)] * inside
        kr = k_buf[:, pl.ds(pl.multiple_of(lax.rem(at + 128, COLS), 128), 128)] * inside
        first_lane = jnp.logical_and(lane == 0, j == 0)
        last_lane = jnp.logical_and(lane == 127, j == last)
        k_left = jnp.where(lane == 0, pltpu.roll(kl, 1, axis=1), pltpu.roll(k, 1, axis=1))
        k_right = jnp.where(lane == 127, pltpu.roll(kr, 127, axis=1), pltpu.roll(k, 127, axis=1))
        k_left = jnp.where(first_lane, 0.0, k_left)
        k_right = jnp.where(last_lane, 0.0, k_right)
        k_above = pltpu.roll(k, 1, axis=0)
        k_below = pltpu.roll(k, EXT - 1, axis=0)
        in_above = pltpu.roll(inside, 1, axis=0) * inside
        in_below = pltpu.roll(inside, EXT - 1, axis=0) * inside
        wa = 0.5 * (k + k_above)
        wb = 0.5 * (k + k_below)
        wl = 0.5 * (k + k_left)
        wr = 0.5 * (k + k_right)
        total = (wa + wb) + (wl + wr)
        for ref, c in ((w_fine, STEP), (w_mid, 4.0 * STEP)):
            ref[0, :, pl.ds(at, 128)] = 1.0 - c * total
            ref[1, :, pl.ds(at, 128)] = c * (wa * in_above)
            ref[2, :, pl.ds(at, 128)] = c * (wb * in_below)
            ref[3, :, pl.ds(at, 128)] = jnp.where(first_lane, 0.0, c * wl)
            ref[4, :, pl.ds(at, 128)] = jnp.where(last_lane, 0.0, c * wr)
        return carry

    lax.fori_loop(0, COLS // 128, weigh, 0)

    def run(src, weights, rows, finish):
        def body(at):
            finish(at, pl.ds(at, WIDTH), stencil(plain(src), weights, at, rows))

        strips(body)

    def store(dst, rows):
        def finish(at, cols, value):
            dst[0:rows, cols] = value

        return finish

    r_halo = {}
    early = []
    early_mate = []
    for p in range(4):
        arrive(halo[p])
        state = i_buf.at[p]
        for j in (1, 2, 3):
            nxt = a_buf.at[p, j - 1]

            def finish(at, cols, value, nxt=nxt, j=j, p=p):
                nxt[:, cols] = value + f_buf[4 * p + j, :, cols]

            run(state, w_fine, EXT, finish)
            state = nxt
        if p < 3:

            def finish(at, cols, value, p=p):
                r_buf[p, 0:ROWS, cols] = (
                    f_buf[4 * p + 4, 0:ROWS, cols] + value - i_buf[p + 1, 0:ROWS, cols]
                )

            run(state, w_fine, ROWS, finish)
            r_halo[p] = edges(r_buf.at[p], r_buf.at[p], t, 3 - p)
            start(r_halo[p])
        else:
            run(state, w_fine, ROWS, store(ahead, ROWS))
        if p == 0:

            def make_g(at):
                cols = pl.ds(at, WIDTH)
                g_buf[:, cols] = f_buf[0, :, cols] - i_buf[0, :, cols]

            strips(make_g)
            early = [remote(g_buf, ge_in, shift(3), s)]
            early_mate = [remote(ppg, ppg, mate, s)]

            @pl.when(core == 0)
            def _():
                start(early)

            run(g_buf, w_mid, EXT, store(pg, EXT))

            @pl.when(core == 0)
            def _():
                run(pg, w_mid, ROWS, store(ppg, ROWS))
                start(early_mate)

    arrive(r_halo[0])
    arrive(r_halo[1])

    def finish_b2(at, cols, value):
        b_buf[0, :, cols] = value + r_buf[1, :, cols]

    run(r_buf.at[0], w_mid, EXT, finish_b2)
    arrive(r_halo[2])

    def finish_b3(at, cols, value):
        b_buf[1, :, cols] = value + r_buf[2, :, cols]

    run(b_buf.at[0], w_mid, EXT, finish_b3)

    def finish_u(at, cols, value):
        u = value + ahead[0:ROWS, cols]
        u_buf[:, cols] = u
        y_buf[core, 0:ROWS, cols] = u + pg[0:ROWS, cols]

    run(b_buf.at[1], w_mid, ROWS, finish_u)

    y_main = [remote(y_buf.at[core, 0:ROWS], y_buf.at[core, 0:ROWS], mate, s)]
    y_edges = edges(y_buf.at[0], y_buf.at[0], t, 1)
    y_cross = edges(y_buf.at[0], y_buf.at[0], mate, 1)
    u_far = edges(u_buf, u_in, shift(3), 4) + [remote(u_buf, u_in.at[0:ROWS], shift(3), s)]

    @pl.when(core == 0)
    def _():
        start(y_edges)
        start(y_cross)

    start(y_main)

    @pl.when(core == 1)
    def _():
        start(u_far)

    def make_base(at):
        cols = pl.ds(at, WIDTH)
        base[0, :, cols] = i_buf[1, 0:ROWS, cols] + r_buf[0, 0:ROWS, cols]
        base[1, :, cols] = i_buf[2, 0:ROWS, cols] + b_buf[0, 0:ROWS, cols]
        base[2, :, cols] = i_buf[3, 0:ROWS, cols] + b_buf[1, 0:ROWS, cols]

    strips(make_base)

    @pl.when(core == 1)
    def _():
        arrive(early)
        arrive(early_mate)
        arrive(y_cross)

    @pl.when(core == 0)
    def _():
        arrive(y_edges)

    arrive(y_main)
    odd = core.astype(jnp.float32)

    def finish_m1(at, cols, value):
        both = value + y_buf[1, 0:ROWS, cols]
        yc[:, cols] = both
        m1[:, cols] = both - odd * ppg[:, cols]

    run(y_buf.at[0], w_mid, ROWS, finish_m1)
    m1_copies = edges(m1, m1_in, shift(2), 2) + [remote(m1, m1_in.at[0:ROWS], shift(2), s)]
    start(m1_copies)

    one = jnp.where(chip >= 1, 1.0, 0.0).astype(jnp.float32)
    two = jnp.where(chip >= 2, 1.0, 0.0).astype(jnp.float32)

    @pl.when(core == 0)
    def _():
        arrive(u_far)
        run(u_in, w_mid, EXT, store(tmp.at[0], EXT))

        def finish_q(at, cols, value):
            q_buf[:, cols] = two * value

        run(tmp.at[0], w_mid, EXT, finish_q)

    @pl.when(core == 1)
    def _():
        q_buf[...] = jnp.zeros_like(q_buf)

    arrive(m1_copies)

    def masked_m1(at, width):
        cols = pl.ds(at, width)
        return one * m1_in[:, cols] + q_buf[:, cols]

    def body_t3(at):
        tmp[1, :, pl.ds(at, WIDTH)] = stencil(masked_m1, w_mid, at, EXT)

    strips(body_t3)

    def finish_m2(at, cols, value):
        m2[:, cols] = value + yc[:, cols]

    run(tmp.at[1], w_mid, ROWS, finish_m2)
    m2_copies = edges(m2, m2_in, shift(4), 3) + [remote(m2, m2_in.at[0:ROWS], shift(4), s)]
    start(m2_copies)
    arrive(m2_copies)

    @pl.when(core == 0)
    def _():
        run(m2_in, w_mid, EXT, store(tmp.at[2], EXT))

        def finish_x(at, cols, value):
            x = g_buf[0:ROWS, cols] + one * m1_in[0:ROWS, cols] + two * value
            x_buf[0:ROWS, cols] = x
            o_buf[0, :, cols] = i_buf[0, 0:ROWS, cols] + x

        run(tmp.at[2], w_mid, ROWS, finish_x)

    @pl.when(core == 1)
    def _():
        def masked_m2(at, width):
            cols = pl.ds(at, width)
            return two * m2_in[:, cols] + one * ge_in[:, cols]

        def body(at):
            tmp[2, :, pl.ds(at, WIDTH)] = stencil(masked_m2, w_mid, at, EXT)

        strips(body)

        def finish_w(at, cols, value):
            tmp[3, :, cols] = value + one * m1_in[:, cols]

        run(tmp.at[2], w_mid, EXT, finish_w)

        def finish_x(at, cols, value):
            x = g_buf[0:ROWS, cols] + y_buf[0, 0:ROWS, cols] + value
            x_buf[0:ROWS, cols] = x
            o_buf[0, :, cols] = i_buf[0, 0:ROWS, cols] + x

        run(tmp.at[3], w_mid, ROWS, finish_x)

    x_copies = edges(x_buf, x_buf, t, 3)
    start(x_copies)
    outs = [pltpu.make_async_copy(o_buf.at[j], out.at[j], out_sem.at[j]) for j in range(4)]
    outs[0].start()
    arrive(x_copies)

    state = x_buf
    for j in (1, 2, 3):
        rows = EXT if j < 3 else ROWS

        def finish_e(at, cols, value, j=j):
            if j < 3:
                e_buf[j - 1, :, cols] = value
            o_buf[j, :, cols] = base[j - 1, :, cols] + value[:ROWS]

        run(state, w_mid, rows, finish_e)
        outs[j].start()
        if j < 3:
            state = e_buf.at[j - 1]

    for c in outs:
        c.wait()
    sent(k_halo)
    for p in range(4):
        sent(halo[p])
        if p < 3:
            sent(r_halo[p])
    sent(y_main)
    sent(m1_copies)
    sent(m2_copies)
    sent(x_copies)

    @pl.when(core == 0)
    def _():
        sent(early)
        sent(early_mate)
        sent(y_edges)
        sent(y_cross)

    @pl.when(core == 1)
    def _():
        sent(u_far)


def per_device(forcing, iterate, permeability):
    def field(*lead, rows=EXT):
        return pltpu.VMEM((*lead, rows, COLS), jnp.float32)

    scratch = [
        field(16),
        field(4),
        field(),
        field(5),
        field(5),
        field(4, 3),
        field(rows=ROWS),
        field(3),
        field(2),
        field(),
        field(),
        field(rows=ROWS),
        field(),
        field(rows=ROWS),
        field(),
        field(2),
        field(rows=ROWS),
        field(rows=ROWS),
        field(),
        field(),
        field(4),
        field(rows=ROWS),
        field(),
        field(),
        field(2),
        field(3, rows=ROWS),
        field(4, rows=ROWS),
        pltpu.SemaphoreType.DMA((NCOPY,)),
        pltpu.SemaphoreType.DMA((NCOPY,)),
        pltpu.SemaphoreType.DMA((9,)),
        pltpu.SemaphoreType.DMA((4,)),
    ]
    return pl.pallas_call(
        kernel,
        name="vcycle",
        out_shape=jax.ShapeDtypeStruct(iterate.shape, iterate.dtype),
        in_specs=[pl.BlockSpec(memory_space=pl.ANY)] * 3,
        out_specs=pl.BlockSpec(memory_space=pl.ANY),
        scratch_shapes=scratch,
        compiler_params=pltpu.CompilerParams(
            collective_id=0, has_side_effects=True, vmem_limit_bytes=40 * 2**20
        ),
    )(forcing, iterate, permeability)


def solution(mesh):
    in_specs = (P("tm", "space", None), P("tm", "space", None), P("space", None))
    out_specs = P("tm", "space", None)
    return jax.shard_map(
        per_device, mesh=mesh, in_specs=in_specs, out_specs=out_specs, check_vma=False
    )
```

```python
import jax
import jax.numpy as jnp
from jax import lax
from jax.experimental import pallas as pl
from jax.experimental.pallas import tpu as pltpu
from jax.sharding import PartitionSpec as P

STEP = 0.06
NT = 128
NS = 4
ROWS = 16
EXT = 24
COLS = 2048
MESH = pl.DeviceIdType.MESH
NCOPY = 112


def apply(v, weights, rows=EXT):
    vl = pltpu.roll(v[:rows], 1, axis=1)
    vr = pltpu.roll(v[:rows], COLS - 1, axis=1)
    above = pltpu.roll(v, 1, axis=0)[:rows]
    below = pltpu.roll(v, EXT - 1, axis=0)[:rows]

    def w(i):
        return weights[i, 0:rows]

    return w(0) * v[:rows] + w(1) * above + w(2) * below + (w(3) * vl + w(4) * vr)


class Batch:
    def __init__(self, core, copies, sender=None, receiver=None):
        self.core, self.copies, self.sender, self.receiver = core, copies, sender, receiver

    def each(self, only, act):
        if only is None:
            for c in self.copies:
                act(c)
        else:

            @pl.when(self.core == only)
            def _():
                for c in self.copies:
                    act(c)

    def start(self):
        self.each(self.sender, lambda c: c.start())

    def arrive(self):
        self.each(self.receiver, lambda c: c.wait_recv())

    def sent(self):
        self.each(self.sender, lambda c: c.wait_send())


def kernel(
    forcing, iterate, perm, out,
    f_buf, i_buf, k_buf, w_fine, w_mid, ahead, r_buf, b_buf, g_buf, pg, ppg, ge_in,
    u_buf, u_in, y_buf, yc, m1, m1_in, q_buf, m2, m2_in, x_buf, base, o_buf,
    send, recv, local, out_sem,
):
    t = lax.axis_index("tm")
    s = lax.axis_index("space")
    core = lax.rem(t, 2)
    chip = t // 2
    up = lax.rem(s + NS - 1, NS)
    down = lax.rem(s + 1, NS)
    mate = t + 1 - 2 * core
    count = [0]
    batches = []

    def shift(by):
        return lax.rem(t + by + NT, NT)

    def remote(src, dst, tm, sp):
        i = count[0]
        count[0] += 1
        return pltpu.make_async_remote_copy(
            src_ref=src, dst_ref=dst, send_sem=send.at[i], recv_sem=recv.at[i],
            device_id=(tm, sp), device_id_type=MESH,
        )

    def edges(src, dst, tm, depth):
        return [
            remote(src.at[0:depth], dst.at[ROWS : ROWS + depth], tm, up),
            remote(src.at[ROWS - depth : ROWS], dst.at[EXT - depth : EXT], tm, down),
        ]

    def batch(copies, sender=None, receiver=None):
        made = Batch(core, copies, sender, receiver)
        batches.append(made)
        made.start()
        return made

    loads = [pltpu.make_async_copy(perm, k_buf.at[0:ROWS], local.at[0])]
    for p in range(4):
        loads.append(pltpu.make_async_copy(iterate.at[p], i_buf.at[p, 0:ROWS], local.at[1 + p]))
        loads.append(
            pltpu.make_async_copy(
                forcing.at[4 * p : 4 * p + 4], f_buf.at[4 * p : 4 * p + 4, 0:ROWS], local.at[5 + p]
            )
        )
    for c in loads:
        c.start()

    barrier = pltpu.get_barrier_semaphore()

    def greet(tm, sp):
        pl.semaphore_signal(barrier, inc=1, device_id=(tm, sp), device_id_type=MESH)

    greet(t, up)
    greet(t, down)
    greet(mate, s)
    for by in (-2, -4):
        for sp in (s, up, down):
            greet(shift(by), sp)

    @pl.when(core == 0)
    def _():
        for sp in (s, up, down):
            greet(shift(-3), sp)

    @pl.when(core == 1)
    def _():
        greet(shift(-3), s)
        for sp in (up, down):
            greet(mate, sp)

    pl.semaphore_wait(barrier, 12)

    k_halo = batch(edges(perm, k_buf, t, 4))
    halo = []
    for p in range(4):
        one = edges(iterate.at[p], i_buf.at[p], t, 4)
        for j in (1, 2, 3):
            one += edges(forcing.at[4 * p + j], f_buf.at[4 * p + j], t, 4 - j)
        if p == 0:
            one += edges(forcing.at[0], f_buf.at[0], t, 3)
        halo.append(batch(one))

    for c in loads:
        c.wait()
    k_halo.arrive()

    row = lax.broadcasted_iota(jnp.int32, (EXT, 128), 0)
    is_below = jnp.logical_and(row >= ROWS, row < ROWS + 4)
    is_above = row >= ROWS + 4
    outside = jnp.logical_or(
        jnp.logical_and(is_below, s == NS - 1), jnp.logical_and(is_above, s == 0)
    )
    inside = jnp.where(outside, 0.0, 1.0).astype(jnp.float32)
    lane = lax.broadcasted_iota(jnp.int32, (EXT, 128), 1)
    in_above = pltpu.roll(inside, 1, axis=0) * inside
    in_below = pltpu.roll(inside, EXT - 1, axis=0) * inside
    for j in range(COLS // 128):
        at = slice(128 * j, 128 * j + 128)
        k = k_buf[:, at] * inside
        zero = jnp.zeros_like(k)
        kl = k_buf[:, 128 * j - 128 : 128 * j] * inside if j else zero
        kr = k_buf[:, 128 * j + 128 : 128 * j + 256] * inside if j < COLS // 128 - 1 else zero
        k_left = jnp.where(lane == 0, pltpu.roll(kl, 1, axis=1), pltpu.roll(k, 1, axis=1))
        k_right = jnp.where(lane == 127, pltpu.roll(kr, 127, axis=1), pltpu.roll(k, 127, axis=1))
        wa = 0.5 * (k + pltpu.roll(k, 1, axis=0))
        wb = 0.5 * (k + pltpu.roll(k, EXT - 1, axis=0))
        wl = 0.5 * (k + k_left)
        wr = 0.5 * (k + k_right)
        total = (wa + wb) + (wl + wr)
        if j == 0:
            wl = jnp.where(lane == 0, 0.0, wl)
        if j == COLS // 128 - 1:
            wr = jnp.where(lane == 127, 0.0, wr)
        for ref, c in ((w_fine, STEP), (w_mid, 4.0 * STEP)):
            ref[0, :, at] = 1.0 - c * total
            ref[1, :, at] = c * (wa * in_above)
            ref[2, :, at] = c * (wb * in_below)
            ref[3, :, at] = c * wl
            ref[4, :, at] = c * wr

    r_halo = []
    for p in range(4):
        halo[p].arrive()
        state = i_buf[p]
        for j in (1, 2, 3):
            state = apply(state, w_fine) + f_buf[4 * p + j]
        last = apply(state, w_fine, ROWS)
        if p < 3:
            r_buf[p, 0:ROWS] = f_buf[4 * p + 4, 0:ROWS] + last - i_buf[p + 1, 0:ROWS]
            r_halo.append(batch(edges(r_buf.at[p], r_buf.at[p], t, 3 - p)))
        else:
            ahead[...] = last
        if p == 0:
            g = f_buf[0] - i_buf[0]
            g_buf[...] = g
            early = batch([remote(g_buf, ge_in, shift(3), s)], 0, 1)
            pg[...] = apply(g, w_mid)

            @pl.when(core == 0)
            def _():
                ppg[...] = apply(pg[...], w_mid, ROWS)

            early_mate = batch([remote(ppg, ppg, mate, s)], 0, 1)

    r_halo[0].arrive()
    r_halo[1].arrive()
    b_buf[0] = apply(r_buf[0], w_mid) + r_buf[1]
    r_halo[2].arrive()
    b_buf[1] = apply(b_buf[0], w_mid) + r_buf[2]
    u = apply(b_buf[1], w_mid, ROWS) + ahead[...]
    u_buf[...] = u
    y_buf[core, 0:ROWS] = u + pg[0:ROWS]

    y_edges = batch(edges(y_buf.at[0], y_buf.at[0], t, 1), 0, 0)
    y_cross = batch(edges(y_buf.at[0], y_buf.at[0], mate, 1), 0, 1)
    y_main = batch([remote(y_buf.at[core, 0:ROWS], y_buf.at[core, 0:ROWS], mate, s)])
    u_far = batch(edges(u_buf, u_in, shift(3), 4) + [remote(u_buf, u_in.at[0:ROWS], shift(3), s)], 1, 0)

    base[0] = i_buf[1, 0:ROWS] + r_buf[0, 0:ROWS]
    base[1] = i_buf[2, 0:ROWS] + b_buf[0, 0:ROWS]
    base[2] = i_buf[3, 0:ROWS] + b_buf[1, 0:ROWS]

    early.arrive()
    early_mate.arrive()
    y_main.arrive()
    y_cross.arrive()
    y_edges.arrive()
    odd = core.astype(jnp.float32)
    both = apply(y_buf[0], w_mid, ROWS) + y_buf[1, 0:ROWS]
    yc[...] = both
    m1[...] = both - odd * ppg[...]
    m1_copies = batch(edges(m1, m1_in, shift(2), 2) + [remote(m1, m1_in.at[0:ROWS], shift(2), s)])

    one = jnp.where(chip >= 1, 1.0, 0.0).astype(jnp.float32)
    two = jnp.where(chip >= 2, 1.0, 0.0).astype(jnp.float32)

    u_far.arrive()

    @pl.when(core == 0)
    def _():
        q_buf[...] = two * apply(apply(u_in[...], w_mid), w_mid)

    @pl.when(core == 1)
    def _():
        q_buf[...] = jnp.zeros_like(q_buf)

    m1_copies.arrive()
    near = one * m1_in[...] + q_buf[...]
    m2[...] = apply(apply(near, w_mid), w_mid, ROWS) + yc[...]
    m2_copies = batch(edges(m2, m2_in, shift(4), 3) + [remote(m2, m2_in.at[0:ROWS], shift(4), s)])
    m2_copies.arrive()

    @pl.when(core == 0)
    def _():
        far = apply(apply(m2_in[...], w_mid), w_mid, ROWS)
        x_buf[0:ROWS] = g_buf[0:ROWS] + one * m1_in[0:ROWS] + two * far

    @pl.when(core == 1)
    def _():
        far = two * m2_in[...] + one * ge_in[...]
        far = apply(apply(far, w_mid), w_mid) + one * m1_in[...]
        x_buf[0:ROWS] = g_buf[0:ROWS] + y_buf[0, 0:ROWS] + apply(far, w_mid, ROWS)

    x_copies = batch(edges(x_buf, x_buf, t, 3))
    outs = [pltpu.make_async_copy(o_buf.at[j], out.at[j], out_sem.at[j]) for j in range(4)]
    o_buf[0] = i_buf[0, 0:ROWS] + x_buf[0:ROWS]
    outs[0].start()
    x_copies.arrive()

    state = x_buf[...]
    for j in (1, 2, 3):
        state = apply(state, w_mid, EXT if j < 3 else ROWS)
        o_buf[j] = base[j - 1] + state[:ROWS]
        outs[j].start()

    for c in outs:
        c.wait()
    for b in batches:
        b.sent()


def per_device(forcing, iterate, permeability):
    def field(*lead, rows=EXT):
        return pltpu.VMEM((*lead, rows, COLS), jnp.float32)

    scratch = [
        field(16),
        field(4),
        field(),
        field(5),
        field(5),
        field(rows=ROWS),
        field(3),
        field(2),
        field(),
        field(),
        field(rows=ROWS),
        field(),
        field(rows=ROWS),
        field(),
        field(2),
        field(rows=ROWS),
        field(rows=ROWS),
        field(),
        field(),
        field(rows=ROWS),
        field(),
        field(),
        field(3, rows=ROWS),
        field(4, rows=ROWS),
        pltpu.SemaphoreType.DMA((NCOPY,)),
        pltpu.SemaphoreType.DMA((NCOPY,)),
        pltpu.SemaphoreType.DMA((9,)),
        pltpu.SemaphoreType.DMA((4,)),
    ]
    return pl.pallas_call(
        kernel,
        name="vcycle",
        out_shape=jax.ShapeDtypeStruct(iterate.shape, iterate.dtype),
        in_specs=[pl.BlockSpec(memory_space=pl.ANY)] * 3,
        out_specs=pl.BlockSpec(memory_space=pl.ANY),
        scratch_shapes=scratch,
        compiler_params=pltpu.CompilerParams(
            collective_id=0, has_side_effects=True, vmem_limit_bytes=40 * 2**20
        ),
    )(forcing, iterate, permeability)


def solution(mesh):
    in_specs = (P("tm", "space", None), P("tm", "space", None), P("space", None))
    out_specs = P("tm", "space", None)
    return jax.shard_map(
        per_device, mesh=mesh, in_specs=in_specs, out_specs=out_specs, check_vma=False
    )
```

```python
import jax
import jax.numpy as jnp
from jax import lax
from jax.experimental import pallas as pl
from jax.experimental.pallas import tpu as pltpu
from jax.sharding import PartitionSpec as P

STEP = 0.06
NT = 128
NS = 4
ROWS = 16
COLS = 2048
HALF = 1024
WIN = 1152
MESH = pl.DeviceIdType.MESH
NCOPY = 48


def apply(v, weights, at=None):
    rows, cols = v.shape
    vl = pltpu.roll(v, 1, axis=1)
    vr = pltpu.roll(v, cols - 1, axis=1)
    above = pltpu.roll(v, 1, axis=0)
    below = pltpu.roll(v, rows - 1, axis=0)

    def w(i):
        return weights[i] if at is None else weights[i, :, pl.ds(at, cols)]

    return w(0) * v + w(1) * above + w(2) * below + (w(3) * vl + w(4) * vr)


def extend(v, rows):
    return jnp.concatenate([v, jnp.zeros((rows - ROWS, v.shape[1]), v.dtype)], axis=0)


def widen(v):
    rim = v[ROWS : ROWS + 8]
    near = lax.broadcasted_iota(jnp.int32, rim.shape, 0) < 4
    zero = jnp.zeros_like(rim)
    return jnp.concatenate([v[0:ROWS], jnp.where(near, rim, zero), jnp.where(near, zero, rim)], axis=0)


def kernel(
    forcing, iterate, perm, out,
    f_buf, i_buf, k_buf, w_fine, w_mid, w_wide, r_buf, b_buf, g_buf, pg, u_buf, cu, cb, cpg, far_src, far_in,
    y_buf, yw, m1_in, m2, m2_in, z_buf, w_buf, x_buf, cx, xh, o_buf,
    send, recv, local, out_sem,
):
    t = lax.axis_index("tm")
    s = lax.axis_index("space")
    core = lax.rem(t, 2)
    chip = t // 2
    up = lax.rem(s + NS - 1, NS)
    down = lax.rem(s + 1, NS)
    mate = t + 1 - 2 * core
    count = [0]
    batches = []

    def shift(by):
        return lax.rem(t + by + NT, NT)

    def remote(src, dst, tm, sp):
        i = count[0]
        count[0] += 1
        return pltpu.make_async_remote_copy(
            src_ref=src, dst_ref=dst, send_sem=send.at[i], recv_sem=recv.at[i],
            device_id=(tm, sp), device_id_type=MESH,
        )

    def batch(copies):
        for c in copies:
            c.start()
        batches.append(copies)
        return copies

    def arrive(copies):
        for c in copies:
            c.wait_recv()

    loads = [
        pltpu.make_async_copy(perm, k_buf.at[0:ROWS], local.at[0]),
        pltpu.make_async_copy(iterate, i_buf, local.at[1]),
        pltpu.make_async_copy(forcing, f_buf, local.at[2]),
    ]
    for c in loads:
        c.start()

    barrier = pltpu.get_barrier_semaphore()
    for tm, sp in ((t, up), (t, down), (mate, s), (shift(-2), s), (shift(-4), s), (shift(-7), s)):
        pl.semaphore_signal(barrier, inc=1, device_id=(tm, sp), device_id_type=MESH)

    m1_in[ROWS + 1 : 23] = jnp.zeros((6, WIN), jnp.float32)
    m2_in[ROWS + 3 : 21] = jnp.zeros((2, WIN), jnp.float32)
    xh[3:5] = jnp.zeros((2, COLS), jnp.float32)
    pl.semaphore_wait(barrier, 6)

    k_halo = batch([
        remote(perm.at[0:8], k_buf.at[16:24], t, up),
        remote(perm.at[8:16], k_buf.at[24:32], t, down),
    ])
    for c in loads:
        c.wait()
    g_buf[...] = f_buf[0] - i_buf[0]
    far = [remote(far_src, far_in, shift(7), s)]
    batches.append(far)

    @pl.when(core == 0)
    def _():
        far_src[...] = g_buf[...]
        far[0].start()

    arrive(k_halo)

    row = lax.broadcasted_iota(jnp.int32, (32, 128), 0)
    is_below = jnp.logical_and(row >= ROWS, row < ROWS + 8)
    is_above = row >= ROWS + 8
    outside = jnp.logical_or(
        jnp.logical_and(is_below, s == NS - 1), jnp.logical_and(is_above, s == 0)
    )
    inside = jnp.where(outside, 0.0, 1.0).astype(jnp.float32)
    lane = lax.broadcasted_iota(jnp.int32, (32, 128), 1)
    in_above = pltpu.roll(inside, 1, axis=0) * inside
    in_below = pltpu.roll(inside, 31, axis=0) * inside
    near = lax.broadcasted_iota(jnp.int32, (8, 128), 0) < 4

    def narrow(v):
        return jnp.concatenate([v[0:ROWS], jnp.where(near, v[16:24], v[24:32])], axis=0)

    for j in range(COLS // 128):
        at = slice(128 * j, 128 * j + 128)
        k = k_buf[:, at] * inside
        zero = jnp.zeros_like(k)
        kl = k_buf[:, 128 * j - 128 : 128 * j] * inside if j else zero
        kr = k_buf[:, 128 * j + 128 : 128 * j + 256] * inside if j < COLS // 128 - 1 else zero
        k_left = jnp.where(lane == 0, pltpu.roll(kl, 1, axis=1), pltpu.roll(k, 1, axis=1))
        k_right = jnp.where(lane == 127, pltpu.roll(kr, 127, axis=1), pltpu.roll(k, 127, axis=1))
        wa = 0.5 * (k + pltpu.roll(k, 1, axis=0))
        wb = 0.5 * (k + pltpu.roll(k, 31, axis=0))
        wl = 0.5 * (k + k_left)
        wr = 0.5 * (k + k_right)
        total = (wa + wb) + (wl + wr)
        wa = wa * in_above
        wb = wb * in_below
        if j == 0:
            wl = jnp.where(lane == 0, 0.0, wl)
        if j == COLS // 128 - 1:
            wr = jnp.where(lane == 127, 0.0, wr)
        for i, v in enumerate((total, wa, wb, wl, wr)):
            fine = 1.0 - STEP * v if i == 0 else STEP * v
            mid = 1.0 - 4.0 * STEP * v if i == 0 else 4.0 * STEP * v
            w_fine[i, :, at] = narrow(fine)
            w_mid[i, :, at] = narrow(mid)
            w_wide[i, :, at] = mid

    pg[...] = apply(extend(g_buf[...], 24), w_mid)
    pg_halo = batch([
        remote(pg.at[16:17], cpg.at[0], t, down),
        remote(pg.at[23:24], cpg.at[1], t, up),
    ])

    for p in range(4):
        state = extend(i_buf[p], 24)
        for j in (1, 2, 3):
            state = apply(state, w_fine) + extend(f_buf[4 * p + j], 24)
        state = apply(state, w_fine)
        if p < 3:
            r_buf[p] = state + extend(f_buf[4 * p + 4] - i_buf[p + 1], 24)
        else:
            r_buf[3] = state

    b_buf[0] = widen(r_buf[0])
    b_buf[1] = apply(b_buf[0], w_wide) + widen(r_buf[1])
    b_buf[2] = apply(b_buf[1], w_wide) + widen(r_buf[2])
    u_buf[...] = apply(b_buf[2], w_wide) + widen(r_buf[3])
    u_rim = batch([
        remote(u_buf.at[16:24], cu.at[0:8], t, down),
        remote(u_buf.at[24:32], cu.at[8:16], t, up),
    ])
    b_rim = []
    for j in range(3):
        b_rim += batch([
            remote(b_buf.at[j, 16:24], cb.at[j, 0:8], t, down),
            remote(b_buf.at[j, 24:32], cb.at[j, 8:16], t, up),
        ])
    arrive(pg_halo)
    pg[0:1] = pg[0:1] + cpg[0]
    pg[15:16] = pg[15:16] + cpg[1]
    arrive(u_rim)
    u = u_buf[0:ROWS] + cu[...]
    y_buf[core] = u + pg[0:ROWS]

    y_swap = batch([remote(y_buf.at[core], y_buf.at[core], mate, s)])

    @pl.when(core == 1)
    def _():
        far_src[...] = u

    arrive(y_swap)

    start = pl.multiple_of(core * (COLS - WIN), 128)
    window = pl.ds(start, WIN)
    yw[...] = apply(extend(y_buf[0, :, window], 24), w_mid, start) + extend(y_buf[1, :, window], 24)
    m1_copies = batch([
        remote(yw.at[0:ROWS], m1_in.at[0:ROWS], shift(2), s),
        remote(yw.at[16:17], m1_in.at[16:17], shift(2), s),
        remote(yw.at[23:24], m1_in.at[23:24], shift(2), s),
    ])

    @pl.when(core == 1)
    def _():
        far[0].start()

    one = jnp.where(chip >= 1, 1.0, 0.0).astype(jnp.float32)
    two = jnp.where(chip >= 2, 1.0, 0.0).astype(jnp.float32)
    arrive(m1_copies)
    m2[...] = one * apply(apply(m1_in[...], w_mid, start), w_mid, start) + yw[...]
    m2_copies = batch([
        remote(m2.at[0:ROWS], m2_in.at[0:ROWS], shift(4), s),
        remote(m2.at[16:19], m2_in.at[16:19], shift(4), s),
        remote(m2.at[21:24], m2_in.at[21:24], shift(4), s),
    ])

    arrive(b_rim)
    for j in range(3):
        o_buf[j + 1] = i_buf[j + 1] + (b_buf[j, 0:ROWS] + cb[j])
    arrive(far)
    use6 = jnp.where(jnp.logical_and(core == 0, chip >= 4), 1.0, 0.0).astype(jnp.float32)
    use7 = jnp.where(jnp.logical_and(core == 1, chip >= 3), -1.0, 0.0).astype(jnp.float32)
    odd = core.astype(jnp.float32)
    z = extend(far_in[...], 32)
    for _ in range(6):
        z = apply(z, w_wide)
    z_buf[...] = use6 * z + use7 * apply(z, w_wide) + extend(g_buf[...] + odd * y_buf[0], 32)
    arrive(m2_copies)
    wide = apply(apply(widen(m2_in[...]), w_wide, start), w_wide, start)
    wide = one * widen(m1_in[...]) + two * wide
    left = wide[:, 0:HALF]
    right = wide[:, WIN - HALF : WIN]

    @pl.when(core == 0)
    def _():
        w_buf[:, 0:HALF] = left

    @pl.when(core == 1)
    def _():
        w_buf[:, HALF:COLS] = right

    half = pl.ds(pl.multiple_of(core * HALF, 128), HALF)
    w_swap = batch([remote(w_buf.at[:, half], w_buf.at[:, half], mate, s)])
    arrive(w_swap)

    @pl.when(core == 0)
    def _():
        x_buf[...] = z_buf[...] + w_buf[...]

    @pl.when(core == 1)
    def _():
        x_buf[...] = z_buf[...] + apply(w_buf[...], w_wide)

    x_rim = batch([
        remote(x_buf.at[16:24], cx.at[0:8], t, down),
        remote(x_buf.at[24:32], cx.at[8:16], t, up),
        remote(x_buf.at[0:3], xh.at[0:3], t, up),
        remote(x_buf.at[13:16], xh.at[5:8], t, down),
    ])
    outs = [pltpu.make_async_copy(o_buf.at[j], out.at[j], out_sem.at[j]) for j in range(4)]
    arrive(x_rim)
    x = x_buf[0:ROWS] + cx[...]
    rim = lax.broadcasted_iota(jnp.int32, (8, COLS), 0) < 4
    state = jnp.concatenate([x, jnp.where(rim, x_buf[16:24], x_buf[24:32]) + xh[...]], axis=0)
    o_buf[0] = i_buf[0] + x
    outs[0].start()

    for j in (1, 2, 3):
        state = apply(state, w_mid)
        o_buf[j] = o_buf[j] + state[0:ROWS]
        outs[j].start()
    for c in outs:
        c.wait()
    for copies in batches:
        for c in copies:
            c.wait_send()


def per_device(forcing, iterate, permeability):
    def field(*shape):
        return pltpu.VMEM(shape, jnp.float32)

    scratch = [
        field(16, ROWS, COLS),
        field(4, ROWS, COLS),
        field(32, COLS),
        field(5, 24, COLS),
        field(5, 24, COLS),
        field(5, 32, COLS),
        field(4, 24, COLS),
        field(3, 32, COLS),
        field(ROWS, COLS),
        field(24, COLS),
        field(32, COLS),
        field(ROWS, COLS),
        field(3, ROWS, COLS),
        field(2, 1, COLS),
        field(ROWS, COLS),
        field(ROWS, COLS),
        field(2, ROWS, COLS),
        field(24, WIN),
        field(24, WIN),
        field(24, WIN),
        field(24, WIN),
        field(32, COLS),
        field(32, COLS),
        field(32, COLS),
        field(ROWS, COLS),
        field(8, COLS),
        field(4, ROWS, COLS),
        pltpu.SemaphoreType.DMA((NCOPY,)),
        pltpu.SemaphoreType.DMA((NCOPY,)),
        pltpu.SemaphoreType.DMA((3,)),
        pltpu.SemaphoreType.DMA((4,)),
    ]
    return pl.pallas_call(
        kernel,
        name="vcycle",
        out_shape=jax.ShapeDtypeStruct(iterate.shape, iterate.dtype),
        in_specs=[pl.BlockSpec(memory_space=pl.ANY)] * 3,
        out_specs=pl.BlockSpec(memory_space=pl.ANY),
        scratch_shapes=scratch,
        compiler_params=pltpu.CompilerParams(
            collective_id=0, has_side_effects=True, vmem_limit_bytes=60 * 2**20
        ),
    )(forcing, iterate, permeability)


def solution(mesh):
    in_specs = (P("tm", "space", None), P("tm", "space", None), P("space", None))
    out_specs = P("tm", "space", None)
    return jax.shard_map(
        per_device, mesh=mesh, in_specs=in_specs, out_specs=out_specs, check_vma=False
    )
```

```python
import jax
import jax.numpy as jnp
from jax import lax
from jax.experimental import pallas as pl
from jax.experimental.pallas import tpu as pltpu
from jax.sharding import PartitionSpec as P

STEP = 0.06
NT = 128
NS = 4
ROWS = 16
COLS = 2048
HALF = 1024
WIN = 1152
MESH = pl.DeviceIdType.MESH
NCOPY = 48


def apply(v, weights, at=None):
    rows, cols = v.shape
    vl = pltpu.roll(v, 1, axis=1)
    vr = pltpu.roll(v, cols - 1, axis=1)
    above = pltpu.roll(v, 1, axis=0)
    below = pltpu.roll(v, rows - 1, axis=0)

    def w(i):
        return weights[i] if at is None else weights[i, :, pl.ds(at, cols)]

    return w(0) * v + w(1) * above + w(2) * below + (w(3) * vl + w(4) * vr)


def extend(v, rows):
    return jnp.concatenate([v, jnp.zeros((rows - ROWS, v.shape[1]), v.dtype)], axis=0)


def widen(v):
    rim = v[ROWS : ROWS + 8]
    near = lax.broadcasted_iota(jnp.int32, rim.shape, 0) < 4
    zero = jnp.zeros_like(rim)
    return jnp.concatenate([v[0:ROWS], jnp.where(near, rim, zero), jnp.where(near, zero, rim)], axis=0)


def kernel(
    forcing, iterate, perm, out,
    f_buf, i_buf, k_buf, w_fine, w_mid, w_wide, s_buf, r_buf, b_buf, g_buf, pg, u_buf, cu, cb, cpg, far_src, far_in,
    y_buf, yw, m1_in, m2, m2_in, z_buf, cz, hz, za, w_buf, cw, hw, w_sum, base,
    send, recv, local,
):
    t = lax.axis_index("tm")
    s = lax.axis_index("space")
    core = lax.rem(t, 2)
    chip = t // 2
    up = lax.rem(s + NS - 1, NS)
    down = lax.rem(s + 1, NS)
    mate = t + 1 - 2 * core
    count = [0]
    batches = []

    def shift(by):
        return lax.rem(t + by + NT, NT)

    def remote(src, dst, tm, sp):
        i = count[0]
        count[0] += 1
        return pltpu.make_async_remote_copy(
            src_ref=src, dst_ref=dst, send_sem=send.at[i], recv_sem=recv.at[i],
            device_id=(tm, sp), device_id_type=MESH,
        )

    def batch(copies):
        for c in copies:
            c.start()
        batches.append(copies)
        return copies

    def arrive(copies):
        for c in copies:
            c.wait_recv()

    loads = [
        pltpu.make_async_copy(perm, k_buf.at[0:ROWS], local.at[0]),
        pltpu.make_async_copy(iterate, i_buf, local.at[1]),
        pltpu.make_async_copy(forcing, f_buf, local.at[2]),
    ]
    for c in loads:
        c.start()

    barrier = pltpu.get_barrier_semaphore()
    for tm, sp in (
        (t, up), (t, down), (mate, s), (mate, up), (mate, down), (shift(-2), s), (shift(-4), s), (shift(-7), s)
    ):
        pl.semaphore_signal(barrier, inc=1, device_id=(tm, sp), device_id_type=MESH)

    m1_in[ROWS + 1 : 23] = jnp.zeros((6, WIN), jnp.float32)
    m2_in[ROWS + 3 : 21] = jnp.zeros((2, WIN), jnp.float32)
    hz[3:5] = jnp.zeros((2, COLS), jnp.float32)
    cw[:, 5:11] = jnp.zeros((2, 6, HALF), jnp.float32)
    pl.semaphore_wait(barrier, 8)

    k_halo = batch([
        remote(perm.at[0:8], k_buf.at[16:24], t, up),
        remote(perm.at[8:16], k_buf.at[24:32], t, down),
    ])
    for c in loads:
        c.wait()
    g_buf[...] = f_buf[0] - i_buf[0]
    far = [remote(far_src, far_in, shift(7), s)]
    batches.append(far)

    @pl.when(core == 0)
    def _():
        far_src[...] = g_buf[...]
        far[0].start()

    arrive(k_halo)

    row = lax.broadcasted_iota(jnp.int32, (32, 128), 0)
    is_below = jnp.logical_and(row >= ROWS, row < ROWS + 8)
    is_above = row >= ROWS + 8
    outside = jnp.logical_or(
        jnp.logical_and(is_below, s == NS - 1), jnp.logical_and(is_above, s == 0)
    )
    inside = jnp.where(outside, 0.0, 1.0).astype(jnp.float32)
    lane = lax.broadcasted_iota(jnp.int32, (32, 128), 1)
    in_above = pltpu.roll(inside, 1, axis=0) * inside
    in_below = pltpu.roll(inside, 31, axis=0) * inside
    near = lax.broadcasted_iota(jnp.int32, (8, 128), 0) < 4

    def narrow(v):
        return jnp.concatenate([v[0:ROWS], jnp.where(near, v[16:24], v[24:32])], axis=0)

    for j in range(COLS // 128):
        at = slice(128 * j, 128 * j + 128)
        k = k_buf[:, at] * inside
        zero = jnp.zeros_like(k)
        kl = k_buf[:, 128 * j - 128 : 128 * j] * inside if j else zero
        kr = k_buf[:, 128 * j + 128 : 128 * j + 256] * inside if j < COLS // 128 - 1 else zero
        k_left = jnp.where(lane == 0, pltpu.roll(kl, 1, axis=1), pltpu.roll(k, 1, axis=1))
        k_right = jnp.where(lane == 127, pltpu.roll(kr, 127, axis=1), pltpu.roll(k, 127, axis=1))
        wa = 0.5 * (k + pltpu.roll(k, 1, axis=0))
        wb = 0.5 * (k + pltpu.roll(k, 31, axis=0))
        wl = 0.5 * (k + k_left)
        wr = 0.5 * (k + k_right)
        total = (wa + wb) + (wl + wr)
        wa = wa * in_above
        wb = wb * in_below
        if j == 0:
            wl = jnp.where(lane == 0, 0.0, wl)
        if j == COLS // 128 - 1:
            wr = jnp.where(lane == 127, 0.0, wr)
        for i, v in enumerate((total, wa, wb, wl, wr)):
            fine = 1.0 - STEP * v if i == 0 else STEP * v
            mid = 1.0 - 4.0 * STEP * v if i == 0 else 4.0 * STEP * v
            w_fine[i, :, at] = narrow(fine)
            w_mid[i, :, at] = narrow(mid)
            w_wide[i, :, at] = mid

    pg[...] = apply(extend(g_buf[...], 24), w_mid)
    pg_halo = batch([
        remote(pg.at[16:17], cpg.at[0], t, down),
        remote(pg.at[23:24], cpg.at[1], t, up),
    ])

    for j in (1, 2, 3, 4):
        for p in range(4):
            state = apply(extend(i_buf[p], 24) if j == 1 else s_buf[j % 2, p], w_fine)
            if j < 4:
                s_buf[1 - j % 2, p] = state + extend(f_buf[4 * p + j], 24)
            elif p < 3:
                r_buf[p] = state + extend(f_buf[4 * p + 4] - i_buf[p + 1], 24)
            else:
                r_buf[3] = state

    b_buf[0] = widen(r_buf[0])
    b_buf[1] = apply(b_buf[0], w_wide) + widen(r_buf[1])
    b_buf[2] = apply(b_buf[1], w_wide) + widen(r_buf[2])
    u_buf[...] = apply(b_buf[2], w_wide) + widen(r_buf[3])
    u_rim = batch([
        remote(u_buf.at[16:24], cu.at[0:8], t, down),
        remote(u_buf.at[24:32], cu.at[8:16], t, up),
    ])
    b_rim = []
    for j in range(3):
        b_rim += batch([
            remote(b_buf.at[j, 16:24], cb.at[j, 0:8], t, down),
            remote(b_buf.at[j, 24:32], cb.at[j, 8:16], t, up),
        ])
    arrive(pg_halo)
    pg[0:1] = pg[0:1] + cpg[0]
    pg[15:16] = pg[15:16] + cpg[1]
    arrive(u_rim)
    u = u_buf[0:ROWS] + cu[...]
    y_buf[core] = u + pg[0:ROWS]

    y_swap = batch([remote(y_buf.at[core], y_buf.at[core], mate, s)])

    @pl.when(core == 1)
    def _():
        far_src[...] = u
        far[0].start()

    arrive(y_swap)

    start = pl.multiple_of(core * (COLS - WIN), 128)
    window = pl.ds(start, WIN)
    yw[...] = apply(extend(y_buf[0, :, window], 24), w_mid, start) + extend(y_buf[1, :, window], 24)
    m1_copies = batch([
        remote(yw.at[0:ROWS], m1_in.at[0:ROWS], shift(2), s),
        remote(yw.at[16:17], m1_in.at[16:17], shift(2), s),
        remote(yw.at[23:24], m1_in.at[23:24], shift(2), s),
    ])

    one = jnp.where(chip >= 1, 1.0, 0.0).astype(jnp.float32)
    two = jnp.where(chip >= 2, 1.0, 0.0).astype(jnp.float32)
    arrive(m1_copies)
    m2[...] = one * apply(apply(m1_in[...], w_mid, start), w_mid, start) + yw[...]
    m2_copies = batch([
        remote(m2.at[0:ROWS], m2_in.at[0:ROWS], shift(4), s),
        remote(m2.at[16:19], m2_in.at[16:19], shift(4), s),
        remote(m2.at[21:24], m2_in.at[21:24], shift(4), s),
    ])

    arrive(b_rim)
    for j in range(3):
        base[j] = i_buf[j + 1] + (b_buf[j, 0:ROWS] + cb[j])
    arrive(far)
    use6 = jnp.where(jnp.logical_and(core == 0, chip >= 4), 1.0, 0.0).astype(jnp.float32)
    use7 = jnp.where(jnp.logical_and(core == 1, chip >= 3), -1.0, 0.0).astype(jnp.float32)
    odd = core.astype(jnp.float32)
    z = extend(far_in[...], 32)
    for _ in range(6):
        z = apply(z, w_wide)
    z_buf[...] = use6 * z + use7 * apply(z, w_wide) + extend(g_buf[...] + odd * y_buf[0], 32)
    z_rim = batch([
        remote(z_buf.at[16:24], cz.at[0:8], t, down),
        remote(z_buf.at[24:32], cz.at[8:16], t, up),
        remote(z_buf.at[0:3], hz.at[0:3], t, up),
        remote(z_buf.at[13:16], hz.at[5:8], t, down),
    ])
    arrive(m2_copies)
    wide = apply(apply(widen(m2_in[...]), w_wide, start), w_wide, start)
    wide = one * widen(m1_in[...]) + two * wide

    @pl.when(core == 0)
    def _():
        w_buf[0] = wide[:, 0:HALF]

    @pl.when(core == 1)
    def _():
        w_buf[1] = wide[:, WIN - HALF : WIN]

    mine = w_buf.at[core]
    w_rim = []
    for tm in (t, mate):
        w_rim += [
            remote(mine.at[16:21], cw.at[core, 0:5], tm, down),
            remote(mine.at[27:32], cw.at[core, 11:16], tm, up),
            remote(mine.at[0:4], hw.at[core, 0:4], tm, up),
            remote(mine.at[12:16], hw.at[core, 4:8], tm, down),
        ]
    w_rim = batch(w_rim)
    w_swap = batch([remote(mine, mine, mate, s)])

    near = lax.broadcasted_iota(jnp.int32, (8, COLS), 0) < 4

    def assemble(own, given, rim):
        return jnp.concatenate(
            [own[0:ROWS] + given, jnp.where(near, own[16:24], own[24:32]) + rim], axis=0
        )

    def halves(ref):
        return jnp.concatenate([ref[0], ref[1]], axis=1)

    arrive(z_rim)
    za[...] = assemble(z_buf[...], cz[...], hz[...])
    arrive(w_swap)
    arrive(w_rim)
    w = assemble(halves(w_buf), halves(cw), halves(hw))

    @pl.when(core == 0)
    def _():
        w_sum[...] = za[...] + w

    @pl.when(core == 1)
    def _():
        w_sum[...] = za[...] + apply(w, w_mid)

    state = w_sum[...]
    out[0] = i_buf[0] + state[0:ROWS]
    for j in (1, 2, 3):
        state = apply(state, w_mid)
        out[j] = base[j - 1] + state[0:ROWS]
    for copies in batches:
        for c in copies:
            c.wait_send()


def per_device(forcing, iterate, permeability):
    def field(*shape):
        return pltpu.VMEM(shape, jnp.float32)

    scratch = [
        field(16, ROWS, COLS),
        field(4, ROWS, COLS),
        field(32, COLS),
        field(5, 24, COLS),
        field(5, 24, COLS),
        field(5, 32, COLS),
        field(2, 4, 24, COLS),
        field(4, 24, COLS),
        field(3, 32, COLS),
        field(ROWS, COLS),
        field(24, COLS),
        field(32, COLS),
        field(ROWS, COLS),
        field(3, ROWS, COLS),
        field(2, 1, COLS),
        field(ROWS, COLS),
        field(ROWS, COLS),
        field(2, ROWS, COLS),
        field(24, WIN),
        field(24, WIN),
        field(24, WIN),
        field(24, WIN),
        field(32, COLS),
        field(ROWS, COLS),
        field(8, COLS),
        field(24, COLS),
        field(2, 32, HALF),
        field(2, ROWS, HALF),
        field(2, 8, HALF),
        field(24, COLS),
        field(3, ROWS, COLS),
        pltpu.SemaphoreType.DMA((NCOPY,)),
        pltpu.SemaphoreType.DMA((NCOPY,)),
        pltpu.SemaphoreType.DMA((3,)),
    ]
    return pl.pallas_call(
        kernel,
        name="vcycle",
        out_shape=jax.ShapeDtypeStruct(iterate.shape, iterate.dtype),
        in_specs=[pl.BlockSpec(memory_space=pltpu.HBM)] * 3,
        out_specs=pl.BlockSpec(memory_space=pltpu.VMEM),
        scratch_shapes=scratch,
        compiler_params=pltpu.CompilerParams(
            collective_id=0, has_side_effects=True, vmem_limit_bytes=int(53.25 * 2**20)
        ),
    )(forcing, iterate, permeability)


def solution(mesh):
    in_specs = (P("tm", "space", None), P("tm", "space", None), P("space", None))
    out_specs = P("tm", "space", None)
    return jax.shard_map(
        per_device, mesh=mesh, in_specs=in_specs, out_specs=out_specs, check_vma=False
    )
```

```python
import jax
import jax.numpy as jnp
from jax import lax
from jax.experimental import pallas as pl
from jax.experimental.pallas import tpu as pltpu
from jax.sharding import PartitionSpec as P

STEP = 0.06
NT = 128
NS = 4
ROWS = 16
COLS = 2048
HALF = 1024
WIN = 1152
MESH = pl.DeviceIdType.MESH
NCOPY = 48


def apply(v, weights, at=None):
    rows, cols = v.shape
    vl = pltpu.roll(v, 1, axis=1)
    vr = pltpu.roll(v, cols - 1, axis=1)
    above = pltpu.roll(v, 1, axis=0)
    below = pltpu.roll(v, rows - 1, axis=0)

    def w(i):
        return weights[i] if at is None else weights[i, :, pl.ds(at, cols)]

    return w(0) * v + w(1) * above + w(2) * below + (w(3) * vl + w(4) * vr)


def extend(v, rows):
    return jnp.concatenate([v, jnp.zeros((rows - ROWS, v.shape[1]), v.dtype)], axis=0)


def widen(v):
    rim = v[ROWS : ROWS + 8]
    near = lax.broadcasted_iota(jnp.int32, rim.shape, 0) < 4
    zero = jnp.zeros_like(rim)
    return jnp.concatenate([v[0:ROWS], jnp.where(near, rim, zero), jnp.where(near, zero, rim)], axis=0)


def kernel(
    forcing, iterate, perm, out,
    f_buf, i_buf, k_buf, w_fine, w_mid, w_wide, s_buf, r_buf, b_buf, g_buf, pg, u_buf, cu, cb, cpg, far_src, far_in,
    y_buf, yw, m1_in, m2, m2_in, z_buf, cz, hz, za, w_buf, cw, hw, w_sum, base,
    send, recv, local,
):
    t = lax.axis_index("tm")
    s = lax.axis_index("space")
    core = lax.rem(t, 2)
    chip = t // 2
    up = lax.rem(s + NS - 1, NS)
    down = lax.rem(s + 1, NS)
    mate = t + 1 - 2 * core
    count = [0]
    batches = []

    def shift(by):
        return lax.rem(t + by + NT, NT)

    def remote(src, dst, tm, sp):
        i = count[0]
        count[0] += 1
        return pltpu.make_async_remote_copy(
            src_ref=src, dst_ref=dst, send_sem=send.at[i], recv_sem=recv.at[i],
            device_id=(tm, sp), device_id_type=MESH,
        )

    def batch(copies, given=None):
        batches.append((copies, given))
        when(given, lambda: [c.start() for c in copies])
        return copies

    def when(given, act):
        if given is None:
            act()
        else:
            pl.when(given)(lambda: (act(), None)[1])

    def arrive(copies, given=None):
        when(given, lambda: [c.wait_recv() for c in copies])

    chips = NT // 2
    has1, has2 = chip >= 1, chip >= 2
    has_far = chip >= 4 - core
    to1, to2 = chip < chips - 1, chip < chips - 2
    to_far = chip < chips - 3 - core

    barrier = pltpu.get_barrier_semaphore()

    def greet(tm, sp):
        pl.semaphore_signal(barrier, inc=1, device_id=(tm, sp), device_id_type=MESH)

    when(has_far, lambda: greet(shift(-7), s))
    when(has2, lambda: greet(shift(-4), s))
    when(has1, lambda: greet(shift(-2), s))
    for tm, sp in ((mate, up), (mate, down), (t, up), (t, down), (mate, s)):
        greet(tm, sp)

    loads = [
        pltpu.make_async_copy(perm, k_buf.at[0:ROWS], local.at[0]),
        pltpu.make_async_copy(iterate, i_buf, local.at[1]),
        pltpu.make_async_copy(forcing, f_buf, local.at[2]),
    ]
    for c in loads:
        c.start()

    m1_in[ROWS + 1 : 23] = jnp.zeros((6, WIN), jnp.float32)
    m2_in[ROWS + 3 : 21] = jnp.zeros((2, WIN), jnp.float32)
    hz[3:5] = jnp.zeros((2, COLS), jnp.float32)
    cw[:, 5:11] = jnp.zeros((2, 6, HALF), jnp.float32)

    @pl.when(jnp.logical_not(has1))
    def _():
        m1_in[...] = jnp.zeros_like(m1_in)

    @pl.when(jnp.logical_not(has2))
    def _():
        m2_in[...] = jnp.zeros_like(m2_in)

    @pl.when(jnp.logical_not(has_far))
    def _():
        far_in[...] = jnp.zeros_like(far_in)

    pl.semaphore_wait(
        barrier, 5 + to1.astype(jnp.int32) + to2.astype(jnp.int32) + to_far.astype(jnp.int32)
    )

    k_halo = batch([
        remote(perm.at[0:8], k_buf.at[16:24], t, up),
        remote(perm.at[8:16], k_buf.at[24:32], t, down),
    ])
    for c in loads:
        c.wait()
    g_buf[...] = f_buf[0] - i_buf[0]
    far = [remote(far_src, far_in, shift(7), s)]
    batches.append((far, to_far))

    @pl.when(jnp.logical_and(core == 0, to_far))
    def _():
        far_src[...] = g_buf[...]
        far[0].start()

    arrive(k_halo)

    row = lax.broadcasted_iota(jnp.int32, (32, 128), 0)
    is_below = jnp.logical_and(row >= ROWS, row < ROWS + 8)
    is_above = row >= ROWS + 8
    outside = jnp.logical_or(
        jnp.logical_and(is_below, s == NS - 1), jnp.logical_and(is_above, s == 0)
    )
    inside = jnp.where(outside, 0.0, 1.0).astype(jnp.float32)
    lane = lax.broadcasted_iota(jnp.int32, (32, 128), 1)
    in_above = pltpu.roll(inside, 1, axis=0) * inside
    in_below = pltpu.roll(inside, 31, axis=0) * inside
    near = lax.broadcasted_iota(jnp.int32, (8, 128), 0) < 4

    def narrow(v):
        return jnp.concatenate([v[0:ROWS], jnp.where(near, v[16:24], v[24:32])], axis=0)

    for j in range(COLS // 128):
        at = slice(128 * j, 128 * j + 128)
        k = k_buf[:, at] * inside
        zero = jnp.zeros_like(k)
        kl = k_buf[:, 128 * j - 128 : 128 * j] * inside if j else zero
        kr = k_buf[:, 128 * j + 128 : 128 * j + 256] * inside if j < COLS // 128 - 1 else zero
        k_left = jnp.where(lane == 0, pltpu.roll(kl, 1, axis=1), pltpu.roll(k, 1, axis=1))
        k_right = jnp.where(lane == 127, pltpu.roll(kr, 127, axis=1), pltpu.roll(k, 127, axis=1))
        wa = 0.5 * (k + pltpu.roll(k, 1, axis=0))
        wb = 0.5 * (k + pltpu.roll(k, 31, axis=0))
        wl = 0.5 * (k + k_left)
        wr = 0.5 * (k + k_right)
        total = (wa + wb) + (wl + wr)
        wa = wa * in_above
        wb = wb * in_below
        if j == 0:
            wl = jnp.where(lane == 0, 0.0, wl)
        if j == COLS // 128 - 1:
            wr = jnp.where(lane == 127, 0.0, wr)
        for i, v in enumerate((total, wa, wb, wl, wr)):
            fine = 1.0 - STEP * v if i == 0 else STEP * v
            mid = 1.0 - 4.0 * STEP * v if i == 0 else 4.0 * STEP * v
            w_fine[i, :, at] = narrow(fine)
            w_mid[i, :, at] = narrow(mid)
            w_wide[i, :, at] = mid

    pg[...] = apply(extend(g_buf[...], 24), w_mid)
    pg_halo = batch([
        remote(pg.at[16:17], cpg.at[0], t, down),
        remote(pg.at[23:24], cpg.at[1], t, up),
    ])

    for j in (1, 2, 3, 4):
        for p in range(4):
            state = apply(extend(i_buf[p], 24) if j == 1 else s_buf[j % 2, p], w_fine)
            if j < 4:
                s_buf[1 - j % 2, p] = state + extend(f_buf[4 * p + j], 24)
            elif p < 3:
                r_buf[p] = state + extend(f_buf[4 * p + 4] - i_buf[p + 1], 24)
            else:
                r_buf[3] = state

    b_buf[0] = widen(r_buf[0])
    b_buf[1] = apply(b_buf[0], w_wide) + widen(r_buf[1])
    b_buf[2] = apply(b_buf[1], w_wide) + widen(r_buf[2])
    u_buf[...] = apply(b_buf[2], w_wide) + widen(r_buf[3])
    u_rim = batch([
        remote(u_buf.at[16:24], cu.at[0:8], t, down),
        remote(u_buf.at[24:32], cu.at[8:16], t, up),
    ])
    b_rim = []
    for j in range(3):
        b_rim += batch([
            remote(b_buf.at[j, 16:24], cb.at[j, 0:8], t, down),
            remote(b_buf.at[j, 24:32], cb.at[j, 8:16], t, up),
        ])
    arrive(pg_halo)
    pg[0:1] = pg[0:1] + cpg[0]
    pg[15:16] = pg[15:16] + cpg[1]
    arrive(u_rim)
    u = u_buf[0:ROWS] + cu[...]
    y_buf[core] = u + pg[0:ROWS]

    y_swap = batch([remote(y_buf.at[core], y_buf.at[core], mate, s)])

    @pl.when(jnp.logical_and(core == 1, to_far))
    def _():
        far_src[...] = u
        far[0].start()

    arrive(y_swap)

    start = pl.multiple_of(core * (COLS - WIN), 128)
    window = pl.ds(start, WIN)
    yw[...] = apply(extend(y_buf[0, :, window], 24), w_mid, start) + extend(y_buf[1, :, window], 24)
    m1_copies = batch([
        remote(yw.at[0:ROWS], m1_in.at[0:ROWS], shift(2), s),
        remote(yw.at[16:17], m1_in.at[16:17], shift(2), s),
        remote(yw.at[23:24], m1_in.at[23:24], shift(2), s),
    ], to1)

    z_rim = [
        remote(z_buf.at[16:24], cz.at[0:8], t, down),
        remote(z_buf.at[24:32], cz.at[8:16], t, up),
        remote(z_buf.at[0:3], hz.at[0:3], t, up),
        remote(z_buf.at[13:16], hz.at[5:8], t, down),
    ]
    batches.append((z_rim, None))

    def far_term(more):
        v = extend(far_in[...], 24)
        for _ in range(4):
            v = apply(v, w_mid)
        v = widen(v)
        for _ in range(more):
            v = apply(v, w_wide)
        return v

    @pl.when(core == 1)
    def _():
        arrive(far, has_far)
        z_buf[...] = extend(g_buf[...] + y_buf[0], 32) - far_term(3)
        for c in z_rim:
            c.start()


    arrive(m1_copies, has1)
    m2[...] = apply(apply(m1_in[...], w_mid, start), w_mid, start) + yw[...]
    m2_copies = batch([
        remote(m2.at[0:ROWS], m2_in.at[0:ROWS], shift(4), s),
        remote(m2.at[16:19], m2_in.at[16:19], shift(4), s),
        remote(m2.at[21:24], m2_in.at[21:24], shift(4), s),
    ], to2)

    arrive(b_rim)
    for j in range(3):
        base[j] = i_buf[j + 1] + (b_buf[j, 0:ROWS] + cb[j])

    @pl.when(core == 0)
    def _():
        arrive(far, has_far)
        z_buf[...] = extend(g_buf[...], 32) + far_term(2)
        for c in z_rim:
            c.start()

    arrive(m2_copies, has2)
    wide = apply(apply(widen(m2_in[...]), w_wide, start), w_wide, start)
    wide = widen(m1_in[...]) + wide

    @pl.when(core == 0)
    def _():
        w_buf[0] = wide[:, 0:HALF]

    @pl.when(core == 1)
    def _():
        w_buf[1] = wide[:, WIN - HALF : WIN]

    mine = w_buf.at[core]
    w_rim = []
    for tm in (t, mate):
        w_rim += [
            remote(mine.at[16:21], cw.at[core, 0:5], tm, down),
            remote(mine.at[27:32], cw.at[core, 11:16], tm, up),
            remote(mine.at[0:4], hw.at[core, 0:4], tm, up),
            remote(mine.at[12:16], hw.at[core, 4:8], tm, down),
        ]
    w_rim = batch(w_rim)
    w_swap = batch([remote(mine, mine, mate, s)])

    near = lax.broadcasted_iota(jnp.int32, (8, COLS), 0) < 4

    def assemble(own, given, rim):
        return jnp.concatenate(
            [own[0:ROWS] + given, jnp.where(near, own[16:24], own[24:32]) + rim], axis=0
        )

    def halves(ref):
        return jnp.concatenate([ref[0], ref[1]], axis=1)

    arrive(z_rim)
    za[...] = assemble(z_buf[...], cz[...], hz[...])
    arrive(w_swap)
    arrive(w_rim)
    w = assemble(halves(w_buf), halves(cw), halves(hw))

    @pl.when(core == 0)
    def _():
        w_sum[...] = za[...] + w

    @pl.when(core == 1)
    def _():
        w_sum[...] = za[...] + apply(w, w_mid)

    state = w_sum[...]
    out[0] = i_buf[0] + state[0:ROWS]
    for j in (1, 2, 3):
        state = apply(state, w_mid)
        out[j] = base[j - 1] + state[0:ROWS]
    for copies, given in batches:
        when(given, lambda: [c.wait_send() for c in copies])


def per_device(forcing, iterate, permeability):
    def field(*shape):
        return pltpu.VMEM(shape, jnp.float32)

    scratch = [
        field(16, ROWS, COLS),
        field(4, ROWS, COLS),
        field(32, COLS),
        field(5, 24, COLS),
        field(5, 24, COLS),
        field(5, 32, COLS),
        field(2, 4, 24, COLS),
        field(4, 24, COLS),
        field(3, 32, COLS),
        field(ROWS, COLS),
        field(24, COLS),
        field(32, COLS),
        field(ROWS, COLS),
        field(3, ROWS, COLS),
        field(2, 1, COLS),
        field(ROWS, COLS),
        field(ROWS, COLS),
        field(2, ROWS, COLS),
        field(24, WIN),
        field(24, WIN),
        field(24, WIN),
        field(24, WIN),
        field(32, COLS),
        field(ROWS, COLS),
        field(8, COLS),
        field(24, COLS),
        field(2, 32, HALF),
        field(2, ROWS, HALF),
        field(2, 8, HALF),
        field(24, COLS),
        field(3, ROWS, COLS),
        pltpu.SemaphoreType.DMA((NCOPY,)),
        pltpu.SemaphoreType.DMA((NCOPY,)),
        pltpu.SemaphoreType.DMA((3,)),
    ]
    return pl.pallas_call(
        kernel,
        name="vcycle",
        out_shape=jax.ShapeDtypeStruct(iterate.shape, iterate.dtype),
        in_specs=[pl.BlockSpec(memory_space=pltpu.HBM)] * 3,
        out_specs=pl.BlockSpec(memory_space=pltpu.VMEM),
        scratch_shapes=scratch,
        compiler_params=pltpu.CompilerParams(
            collective_id=0, has_side_effects=True, vmem_limit_bytes=int(53.25 * 2**20)
        ),
    )(forcing, iterate, permeability)


def solution(mesh):
    in_specs = (P("tm", "space", None), P("tm", "space", None), P("space", None))
    out_specs = P("tm", "space", None)
    return jax.shard_map(
        per_device, mesh=mesh, in_specs=in_specs, out_specs=out_specs, check_vma=False
    )
```

```python
import jax
import jax.numpy as jnp
from jax import lax
from jax.experimental import pallas as pl
from jax.experimental.pallas import tpu as pltpu
from jax.sharding import PartitionSpec as P

STEP = 0.06
NT = 128
NS = 4
ROWS = 16
COLS = 2048
HALF = 1024
WIN = 1152
MESH = pl.DeviceIdType.MESH
NCOPY = 48


def apply(v, weights, at=None):
    rows, cols = v.shape
    vl = pltpu.roll(v, 1, axis=1)
    vr = pltpu.roll(v, cols - 1, axis=1)
    above = pltpu.roll(v, 1, axis=0)
    below = pltpu.roll(v, rows - 1, axis=0)

    def w(i):
        return weights[i] if at is None else weights[i, :, pl.ds(at, cols)]

    return w(0) * v + w(1) * above + w(2) * below + (w(3) * vl + w(4) * vr)


def extend(v, rows):
    return jnp.concatenate([v, jnp.zeros((rows - ROWS, v.shape[1]), v.dtype)], axis=0)


def widen(v):
    rim = v[ROWS : ROWS + 8]
    near = lax.broadcasted_iota(jnp.int32, rim.shape, 0) < 4
    zero = jnp.zeros_like(rim)
    return jnp.concatenate([v[0:ROWS], jnp.where(near, rim, zero), jnp.where(near, zero, rim)], axis=0)


def kernel(
    forcing, iterate, perm, out,
    f_buf, i_buf, k_buf, w_fine, w_mid, w_wide, s_buf, r_buf, b_buf, g_buf, pg, u_buf, cu, cb, cpg, far_src, far_in,
    y_buf, yw, m1_in, m2, m2_in, z_buf, cz, hz, za, w_buf, cw, hw, w_sum, base,
    send, recv, local,
):
    t = lax.axis_index("tm")
    s = lax.axis_index("space")
    core = lax.rem(t, 2)
    chip = t // 2
    up = lax.rem(s + NS - 1, NS)
    down = lax.rem(s + 1, NS)
    mate = t + 1 - 2 * core
    count = [0]
    batches = []

    chips = NT // 2
    has_up, has_down = s > 0, s < NS - 1
    has1, has2 = chip >= 1, chip >= 2
    has_far = chip >= 4 - core
    to1, to2 = chip < chips - 1, chip < chips - 2
    to_far = chip < chips - 3 - core

    def shift(by):
        return lax.rem(t + by + NT, NT)

    def remote(src, dst, tm, sp, sends=None, receives=None):
        i = count[0]
        count[0] += 1
        copy = pltpu.make_async_remote_copy(
            src_ref=src, dst_ref=dst, send_sem=send.at[i], recv_sem=recv.at[i],
            device_id=(tm, sp), device_id_type=MESH,
        )
        return copy, sends, receives

    def upward(src, dst, tm=t):
        return remote(src, dst, tm, up, has_up, has_down)

    def downward(src, dst, tm=t):
        return remote(src, dst, tm, down, has_down, has_up)

    def when(given, act):
        if given is None:
            act()
        else:

            @pl.when(given)
            def _():
                act()

    def each(copies, which, act):
        groups = []
        for c in copies:
            same = [g for g in groups if g[0] is c[which]]
            if same:
                same[0][1].append(c[0])
            else:
                groups.append((c[which], [c[0]]))
        for given, members in groups:
            when(given, lambda: [act(c) for c in members])

    def begin(copies):
        each(copies, 1, lambda c: c.start())

    def batch(copies):
        batches.append(copies)
        begin(copies)
        return copies

    def arrive(copies):
        each(copies, 2, lambda c: c.wait_recv())

    barrier = pltpu.get_barrier_semaphore()

    def greet(tm, sp):
        pl.semaphore_signal(barrier, inc=1, device_id=(tm, sp), device_id_type=MESH)

    when(has_far, lambda: greet(shift(-7), s))
    when(has2, lambda: greet(shift(-4), s))
    when(has1, lambda: greet(shift(-2), s))
    when(has_up, lambda: [greet(tm, up) for tm in (mate, t)])
    when(has_down, lambda: [greet(tm, down) for tm in (mate, t)])
    greet(mate, s)

    loads = [
        pltpu.make_async_copy(perm, k_buf.at[0:ROWS], local.at[0]),
        pltpu.make_async_copy(iterate, i_buf, local.at[1]),
        pltpu.make_async_copy(forcing, f_buf, local.at[2]),
    ]
    for c in loads:
        c.start()

    m1_in[ROWS + 1 : 23] = jnp.zeros((6, WIN), jnp.float32)
    m2_in[ROWS + 3 : 21] = jnp.zeros((2, WIN), jnp.float32)
    hz[3:5] = jnp.zeros((2, COLS), jnp.float32)
    cw[:, 5:11] = jnp.zeros((2, 6, HALF), jnp.float32)

    def clear(ref):
        ref[...] = jnp.zeros(ref.shape, jnp.float32)

    when(jnp.logical_not(has1), lambda: clear(m1_in))
    when(jnp.logical_not(has2), lambda: clear(m2_in))
    when(jnp.logical_not(has_far), lambda: clear(far_in))

    @pl.when(s == 0)
    def _():
        for ref in (
            k_buf.at[24:32], cpg.at[0], cu.at[0:8], cb.at[:, 0:8], cz.at[0:8], hz, cw.at[:, 0:5], hw.at[:, 4:8]
        ):
            clear(ref)

    @pl.when(s == NS - 1)
    def _():
        for ref in (
            k_buf.at[16:24], cpg.at[1], cu.at[8:16], cb.at[:, 8:16], cz.at[8:16], hz, cw.at[:, 11:16], hw.at[:, 0:4]
        ):
            clear(ref)

    def number(given, times=1):
        return jnp.where(given, times, 0).astype(jnp.int32)

    pl.semaphore_wait(
        barrier,
        1 + number(has_up, 2) + number(has_down, 2) + number(to1) + number(to2) + number(to_far),
    )

    k_halo = batch([
        upward(perm.at[0:8], k_buf.at[16:24]),
        downward(perm.at[8:16], k_buf.at[24:32]),
    ])
    for c in loads:
        c.wait()
    g_buf[...] = f_buf[0] - i_buf[0]
    far = [remote(far_src, far_in, shift(7), s, to_far, has_far)]
    batches.append(far)

    @pl.when(jnp.logical_and(core == 0, to_far))
    def _():
        far_src[...] = g_buf[...]
        far[0][0].start()

    arrive(k_halo)

    row = lax.broadcasted_iota(jnp.int32, (32, 128), 0)
    is_below = jnp.logical_and(row >= ROWS, row < ROWS + 8)
    is_above = row >= ROWS + 8
    outside = jnp.logical_or(
        jnp.logical_and(is_below, s == NS - 1), jnp.logical_and(is_above, s == 0)
    )
    inside = jnp.where(outside, 0.0, 1.0).astype(jnp.float32)
    lane = lax.broadcasted_iota(jnp.int32, (32, 128), 1)
    in_above = pltpu.roll(inside, 1, axis=0) * inside
    in_below = pltpu.roll(inside, 31, axis=0) * inside
    near = lax.broadcasted_iota(jnp.int32, (8, 128), 0) < 4

    def narrow(v):
        return jnp.concatenate([v[0:ROWS], jnp.where(near, v[16:24], v[24:32])], axis=0)

    for j in range(COLS // 128):
        at = slice(128 * j, 128 * j + 128)
        k = k_buf[:, at] * inside
        zero = jnp.zeros_like(k)
        kl = k_buf[:, 128 * j - 128 : 128 * j] * inside if j else zero
        kr = k_buf[:, 128 * j + 128 : 128 * j + 256] * inside if j < COLS // 128 - 1 else zero
        k_left = jnp.where(lane == 0, pltpu.roll(kl, 1, axis=1), pltpu.roll(k, 1, axis=1))
        k_right = jnp.where(lane == 127, pltpu.roll(kr, 127, axis=1), pltpu.roll(k, 127, axis=1))
        wa = 0.5 * (k + pltpu.roll(k, 1, axis=0))
        wb = 0.5 * (k + pltpu.roll(k, 31, axis=0))
        wl = 0.5 * (k + k_left)
        wr = 0.5 * (k + k_right)
        total = (wa + wb) + (wl + wr)
        wa = wa * in_above
        wb = wb * in_below
        if j == 0:
            wl = jnp.where(lane == 0, 0.0, wl)
        if j == COLS // 128 - 1:
            wr = jnp.where(lane == 127, 0.0, wr)
        for i, v in enumerate((total, wa, wb, wl, wr)):
            fine = 1.0 - STEP * v if i == 0 else STEP * v
            mid = 1.0 - 4.0 * STEP * v if i == 0 else 4.0 * STEP * v
            w_fine[i, :, at] = narrow(fine)
            w_mid[i, :, at] = narrow(mid)
            w_wide[i, :, at] = mid

    pg[...] = apply(extend(g_buf[...], 24), w_mid)
    pg_halo = batch([
        downward(pg.at[16:17], cpg.at[0]),
        upward(pg.at[23:24], cpg.at[1]),
    ])

    for j in (1, 2, 3, 4):
        for p in range(4):
            state = apply(extend(i_buf[p], 24) if j == 1 else s_buf[j % 2, p], w_fine)
            if j < 4:
                s_buf[1 - j % 2, p] = state + extend(f_buf[4 * p + j], 24)
            elif p < 3:
                r_buf[p] = state + extend(f_buf[4 * p + 4] - i_buf[p + 1], 24)
            else:
                r_buf[3] = state

    b_buf[0] = widen(r_buf[0])
    b_buf[1] = apply(b_buf[0], w_wide) + widen(r_buf[1])
    b_buf[2] = apply(b_buf[1], w_wide) + widen(r_buf[2])
    u_buf[...] = apply(b_buf[2], w_wide) + widen(r_buf[3])
    u_rim = batch([
        downward(u_buf.at[16:24], cu.at[0:8]),
        upward(u_buf.at[24:32], cu.at[8:16]),
    ])
    b_rim = []
    for j in range(3):
        b_rim += batch([
            downward(b_buf.at[j, 16:24], cb.at[j, 0:8]),
            upward(b_buf.at[j, 24:32], cb.at[j, 8:16]),
        ])
    arrive(pg_halo)
    pg[0:1] = pg[0:1] + cpg[0]
    pg[15:16] = pg[15:16] + cpg[1]
    arrive(u_rim)
    u = u_buf[0:ROWS] + cu[...]
    y_buf[core] = u + pg[0:ROWS]

    y_swap = batch([remote(y_buf.at[core], y_buf.at[core], mate, s)])

    @pl.when(jnp.logical_and(core == 1, to_far))
    def _():
        far_src[...] = u
        far[0][0].start()

    arrive(y_swap)

    start = pl.multiple_of(core * (COLS - WIN), 128)
    window = pl.ds(start, WIN)
    yw[...] = apply(extend(y_buf[0, :, window], 24), w_mid, start) + extend(y_buf[1, :, window], 24)
    m1_copies = batch([
        remote(yw.at[0:ROWS], m1_in.at[0:ROWS], shift(2), s, to1, has1),
        remote(yw.at[16:17], m1_in.at[16:17], shift(2), s, to1, has1),
        remote(yw.at[23:24], m1_in.at[23:24], shift(2), s, to1, has1),
    ])

    z_rim = [
        downward(z_buf.at[16:24], cz.at[0:8]),
        upward(z_buf.at[24:32], cz.at[8:16]),
        upward(z_buf.at[0:3], hz.at[0:3]),
        downward(z_buf.at[13:16], hz.at[5:8]),
    ]
    batches.append(z_rim)

    def far_term(more):
        v = extend(far_in[...], 24)
        for _ in range(4):
            v = apply(v, w_mid)
        v = widen(v)
        for _ in range(more):
            v = apply(v, w_wide)
        return v

    @pl.when(core == 1)
    def _():
        arrive(far)
        z_buf[...] = extend(g_buf[...] + y_buf[0], 32) - far_term(3)
        begin(z_rim)


    arrive(m1_copies)
    m2[...] = apply(apply(m1_in[...], w_mid, start), w_mid, start) + yw[...]
    m2_copies = batch([
        remote(m2.at[0:ROWS], m2_in.at[0:ROWS], shift(4), s, to2, has2),
        remote(m2.at[16:19], m2_in.at[16:19], shift(4), s, to2, has2),
        remote(m2.at[21:24], m2_in.at[21:24], shift(4), s, to2, has2),
    ])

    arrive(b_rim)
    for j in range(3):
        base[j] = i_buf[j + 1] + (b_buf[j, 0:ROWS] + cb[j])

    @pl.when(core == 0)
    def _():
        arrive(far)
        z_buf[...] = extend(g_buf[...], 32) + far_term(2)
        begin(z_rim)

    arrive(m2_copies)
    wide = apply(apply(widen(m2_in[...]), w_wide, start), w_wide, start)
    wide = widen(m1_in[...]) + wide

    @pl.when(core == 0)
    def _():
        w_buf[0] = wide[:, 0:HALF]

    @pl.when(core == 1)
    def _():
        w_buf[1] = wide[:, WIN - HALF : WIN]

    mine = w_buf.at[core]
    w_rim = []
    for tm in (t, mate):
        w_rim += [
            downward(mine.at[16:21], cw.at[core, 0:5], tm),
            upward(mine.at[27:32], cw.at[core, 11:16], tm),
            upward(mine.at[0:4], hw.at[core, 0:4], tm),
            downward(mine.at[12:16], hw.at[core, 4:8], tm),
        ]
    w_rim = batch(w_rim)
    w_swap = batch([remote(mine, mine, mate, s)])

    near = lax.broadcasted_iota(jnp.int32, (8, COLS), 0) < 4

    def assemble(own, given, rim):
        return jnp.concatenate(
            [own[0:ROWS] + given, jnp.where(near, own[16:24], own[24:32]) + rim], axis=0
        )

    def halves(ref):
        return jnp.concatenate([ref[0], ref[1]], axis=1)

    arrive(z_rim)
    za[...] = assemble(z_buf[...], cz[...], hz[...])
    arrive(w_swap)
    arrive(w_rim)
    w = assemble(halves(w_buf), halves(cw), halves(hw))

    @pl.when(core == 0)
    def _():
        w_sum[...] = za[...] + w

    @pl.when(core == 1)
    def _():
        w_sum[...] = za[...] + apply(w, w_mid)

    state = w_sum[...]
    out[0] = i_buf[0] + state[0:ROWS]
    for j in (1, 2, 3):
        state = apply(state, w_mid)
        out[j] = base[j - 1] + state[0:ROWS]
    for copies in batches:
        each(copies, 1, lambda c: c.wait_send())


def per_device(forcing, iterate, permeability):
    def field(*shape):
        return pltpu.VMEM(shape, jnp.float32)

    scratch = [
        field(16, ROWS, COLS),
        field(4, ROWS, COLS),
        field(32, COLS),
        field(5, 24, COLS),
        field(5, 24, COLS),
        field(5, 32, COLS),
        field(2, 4, 24, COLS),
        field(4, 24, COLS),
        field(3, 32, COLS),
        field(ROWS, COLS),
        field(24, COLS),
        field(32, COLS),
        field(ROWS, COLS),
        field(3, ROWS, COLS),
        field(2, 1, COLS),
        field(ROWS, COLS),
        field(ROWS, COLS),
        field(2, ROWS, COLS),
        field(24, WIN),
        field(24, WIN),
        field(24, WIN),
        field(24, WIN),
        field(32, COLS),
        field(ROWS, COLS),
        field(8, COLS),
        field(24, COLS),
        field(2, 32, HALF),
        field(2, ROWS, HALF),
        field(2, 8, HALF),
        field(24, COLS),
        field(3, ROWS, COLS),
        pltpu.SemaphoreType.DMA((NCOPY,)),
        pltpu.SemaphoreType.DMA((NCOPY,)),
        pltpu.SemaphoreType.DMA((3,)),
    ]
    return pl.pallas_call(
        kernel,
        name="vcycle",
        out_shape=pltpu.VMEM(iterate.shape, iterate.dtype),
        in_specs=[pl.BlockSpec(memory_space=pltpu.HBM)] * 3,
        out_specs=pl.BlockSpec(memory_space=pltpu.VMEM),
        scratch_shapes=scratch,
        compiler_params=pltpu.CompilerParams(
            collective_id=0, has_side_effects=True, vmem_limit_bytes=24 * 2**20
        ),
    )(*(pltpu.with_memory_space_constraint(v, pltpu.HBM) for v in (forcing, iterate, permeability)))


def solution(mesh):
    in_specs = (P("tm", "space", None), P("tm", "space", None), P("space", None))
    out_specs = P("tm", "space", None)
    return jax.shard_map(
        per_device, mesh=mesh, in_specs=in_specs, out_specs=out_specs, check_vma=False
    )
```

```python
import jax
import jax.numpy as jnp
from jax import lax
from jax.experimental import pallas as pl
from jax.experimental.pallas import tpu as pltpu
from jax.sharding import PartitionSpec as P

STEP = 0.06
NT = 128
NS = 4
ROWS = 16
COLS = 2048
HALF = 1024
WIN = 1152
MESH = pl.DeviceIdType.MESH
NCOPY = 48


def apply(v, weights, at=None):
    rows, cols = v.shape
    vl = pltpu.roll(v, 1, axis=1)
    vr = pltpu.roll(v, cols - 1, axis=1)
    above = pltpu.roll(v, 1, axis=0)
    below = pltpu.roll(v, rows - 1, axis=0)

    def w(i):
        return weights[i] if at is None else weights[i, :, pl.ds(at, cols)]

    return w(0) * v + w(1) * above + w(2) * below + (w(3) * vl + w(4) * vr)


def extend(v, rows):
    return jnp.concatenate([v, jnp.zeros((rows - ROWS, v.shape[1]), v.dtype)], axis=0)


def widen(v):
    rim = v[ROWS : ROWS + 8]
    near = lax.broadcasted_iota(jnp.int32, rim.shape, 0) < 4
    zero = jnp.zeros_like(rim)
    return jnp.concatenate([v[0:ROWS], jnp.where(near, rim, zero), jnp.where(near, zero, rim)], axis=0)


def kernel(
    forcing, iterate, perm, out,
    f_buf, i_buf, k_buf, k_near_buf, w_fine, w_mid, w_wide, s_buf, r_buf, b_buf, g_buf, pg, u_buf, cu, cb, cpg, far_src, far_in,
    y_buf, yw, m1_in, m2, m2_in, z_buf, cz, hz, za, w_buf, cw, hw, w_sum, base,
    send, recv, local,
):
    t = lax.axis_index("tm")
    s = lax.axis_index("space")
    core = lax.rem(t, 2)
    chip = t // 2
    up = lax.rem(s + NS - 1, NS)
    down = lax.rem(s + 1, NS)
    mate = t + 1 - 2 * core
    count = [0]
    batches = []

    chips = NT // 2
    has_up, has_down = s > 0, s < NS - 1
    has1, has2 = chip >= 1, chip >= 2
    has_far = chip >= 4 - core
    to1, to2 = chip < chips - 1, chip < chips - 2
    to_far = chip < chips - 3 - core

    def shift(by):
        return lax.rem(t + by + NT, NT)

    def remote(src, dst, tm, sp, sends=None, receives=None):
        i = count[0]
        count[0] += 1
        copy = pltpu.make_async_remote_copy(
            src_ref=src, dst_ref=dst, send_sem=send.at[i], recv_sem=recv.at[i],
            device_id=(tm, sp), device_id_type=MESH,
        )
        return copy, sends, receives

    def upward(src, dst, tm=t):
        return remote(src, dst, tm, up, has_up, has_down)

    def downward(src, dst, tm=t):
        return remote(src, dst, tm, down, has_down, has_up)

    def when(given, act):
        if given is None:
            act()
        else:

            @pl.when(given)
            def _():
                act()

    def each(copies, which, act):
        groups = []
        for c in copies:
            same = [g for g in groups if g[0] is c[which]]
            if same:
                same[0][1].append(c[0])
            else:
                groups.append((c[which], [c[0]]))
        for given, members in groups:
            when(given, lambda: [act(c) for c in members])

    def begin(copies):
        each(copies, 1, lambda c: c.start())

    def batch(copies):
        batches.append(copies)
        begin(copies)
        return copies

    def arrive(copies):
        each(copies, 2, lambda c: c.wait_recv())

    barrier = pltpu.get_barrier_semaphore()

    def greet(tm, sp):
        pl.semaphore_signal(barrier, inc=1, device_id=(tm, sp), device_id_type=MESH)

    when(has_far, lambda: greet(shift(-7), s))
    when(has2, lambda: greet(shift(-4), s))
    when(has1, lambda: greet(shift(-2), s))
    when(has_up, lambda: [greet(tm, up) for tm in (mate, t)])
    when(has_down, lambda: [greet(tm, down) for tm in (mate, t)])
    greet(mate, s)

    loads = [
        pltpu.make_async_copy(perm, k_buf.at[0:ROWS], local.at[0]),
        pltpu.make_async_copy(iterate, i_buf, local.at[1]),
        pltpu.make_async_copy(forcing, f_buf, local.at[2]),
    ]
    for c in loads:
        c.start()

    m1_in[ROWS + 1 : 23] = jnp.zeros((6, WIN), jnp.float32)
    m2_in[ROWS + 3 : 21] = jnp.zeros((2, WIN), jnp.float32)
    hz[3:5] = jnp.zeros((2, COLS), jnp.float32)
    cw[:, 5:11] = jnp.zeros((2, 6, HALF), jnp.float32)

    def clear(ref):
        ref[...] = jnp.zeros(ref.shape, jnp.float32)

    when(jnp.logical_not(has1), lambda: clear(m1_in))
    when(jnp.logical_not(has2), lambda: clear(m2_in))
    when(jnp.logical_not(has_far), lambda: clear(far_in))

    @pl.when(s == 0)
    def _():
        for ref in (
            k_buf.at[24:32], k_near_buf.at[4:8], cpg.at[0], cu.at[0:8], cb.at[:, 0:8], cz.at[0:8], hz, cw.at[:, 0:5], hw.at[:, 4:8]
        ):
            clear(ref)

    @pl.when(s == NS - 1)
    def _():
        for ref in (
            k_buf.at[16:24], k_near_buf.at[0:4], cpg.at[1], cu.at[8:16], cb.at[:, 8:16], cz.at[8:16], hz, cw.at[:, 11:16], hw.at[:, 0:4]
        ):
            clear(ref)

    def number(given, times=1):
        return jnp.where(given, times, 0).astype(jnp.int32)

    pl.semaphore_wait(
        barrier,
        1 + number(has_up, 2) + number(has_down, 2) + number(to1) + number(to2) + number(to_far),
    )

    k_near = batch([
        upward(perm.at[0:4], k_near_buf.at[0:4]),
        downward(perm.at[12:16], k_near_buf.at[4:8]),
    ])
    k_far = batch([
        upward(perm.at[0:8], k_buf.at[16:24]),
        downward(perm.at[8:16], k_buf.at[24:32]),
    ])
    for c in loads:
        c.wait()
    g_buf[...] = f_buf[0] - i_buf[0]
    far = [remote(far_src, far_in, shift(7), s, to_far, has_far)]
    batches.append(far)

    @pl.when(jnp.logical_and(core == 0, to_far))
    def _():
        far_src[...] = g_buf[...]
        far[0][0].start()

    lane = lax.broadcasted_iota(jnp.int32, (1, 128), 1)
    tiles = COLS // 128

    def sides(part, j):
        k = part(j)
        zero = jnp.zeros_like(k)
        kl = pltpu.roll(part(j - 1), 1, axis=1) if j else zero
        kr = pltpu.roll(part(j + 1), 127, axis=1) if j < tiles - 1 else zero
        left = 0.5 * (k + jnp.where(lane == 0, kl, pltpu.roll(k, 1, axis=1)))
        right = 0.5 * (k + jnp.where(lane == 127, kr, pltpu.roll(k, 127, axis=1)))
        return k, left, right

    def closed(left, right, j):
        if j == 0:
            left = jnp.where(lane == 0, 0.0, left)
        if j == tiles - 1:
            right = jnp.where(lane == 127, 0.0, right)
        return left, right

    own_row = lax.broadcasted_iota(jnp.int32, (ROWS, 128), 0)
    for j in range(tiles):
        at = slice(128 * j, 128 * j + 128)
        k, wl, wr = sides(lambda i: k_buf[0:ROWS, 128 * i : 128 * i + 128], j)
        k_above = jnp.where(own_row == 0, 0.0, pltpu.roll(k, 1, axis=0))
        k_below = jnp.where(own_row == ROWS - 1, 0.0, pltpu.roll(k, ROWS - 1, axis=0))
        wa = 0.5 * (k + k_above)
        wb = 0.5 * (k + k_below)
        total = (wa + wb) + (wl + wr)
        wl, wr = closed(wl, wr, j)
        for ref, c in ((w_fine, STEP), (w_mid, 4.0 * STEP)):
            ref[0, 0:ROWS, at] = 1.0 - c * total
            ref[1, 0:ROWS, at] = c * wa
            ref[2, 0:ROWS, at] = c * wb
            ref[3, 0:ROWS, at] = c * wl
            ref[4, 0:ROWS, at] = c * wr

    rim_row = lax.broadcasted_iota(jnp.int32, (8, 128), 0)
    low = jnp.where(s < NS - 1, 1.0, 0.0).astype(jnp.float32)
    high = jnp.where(s > 0, 1.0, 0.0).astype(jnp.float32)

    def rim_weights(part, j, inside, first_above, last_below):
        k, wl, wr = sides(part, j)
        wa = 0.5 * (k + jnp.where(rim_row == 0, first_above, pltpu.roll(k, 1, axis=0)))
        wb = 0.5 * (k + jnp.where(rim_row == 7, last_below, pltpu.roll(k, 7, axis=0)))
        total = (wa + wb) + (wl + wr)
        wl, wr = closed(wl, wr, j)
        return total, inside * wa, inside * wb, wl, wr

    arrive(k_near)
    near = rim_row < 4
    inside = jnp.where(near, low, high)
    for j in range(tiles):
        at = slice(128 * j, 128 * j + 128)

        def part(i):
            return inside * k_near_buf[:, 128 * i : 128 * i + 128]

        top, bottom = k_buf[0:1, at], k_buf[15:16, at]
        rim = part(j)
        weights = rim_weights(part, j, inside, bottom, top)
        for ref, c in ((w_fine, STEP), (w_mid, 4.0 * STEP)):
            ref[0, ROWS:24, at] = 1.0 - c * weights[0]
            for i in (1, 2, 3, 4):
                ref[i, ROWS:24, at] = c * weights[i]
            ref[0, 0:1, at] = ref[0, 0:1, at] - (0.5 * c) * rim[7:8]
            ref[1, 0:1, at] = (high * 0.5 * c) * (top + rim[7:8])
            ref[0, 15:16, at] = ref[0, 15:16, at] - (0.5 * c) * rim[0:1]
            ref[2, 15:16, at] = (low * 0.5 * c) * (bottom + rim[0:1])

    pg[...] = apply(extend(g_buf[...], 24), w_mid)
    pg_halo = batch([
        downward(pg.at[16:17], cpg.at[0]),
        upward(pg.at[23:24], cpg.at[1]),
    ])

    for j in (1, 2, 3, 4):
        for p in range(4):
            state = apply(extend(i_buf[p], 24) if j == 1 else s_buf[j % 2, p], w_fine)
            if j < 4:
                s_buf[1 - j % 2, p] = state + extend(f_buf[4 * p + j], 24)
            elif p < 3:
                r_buf[p] = state + extend(f_buf[4 * p + 4] - i_buf[p + 1], 24)
            else:
                r_buf[3] = state

    arrive(k_far)
    for j in range(tiles):
        at = slice(128 * j, 128 * j + 128)
        for lo, inside in ((16, low), (24, high)):

            def part(i):
                return inside * k_buf[lo : lo + 8, 128 * i : 128 * i + 128]

            above = k_buf[15:16, at] if lo == 16 else jnp.zeros((1, 128), jnp.float32)
            below = k_buf[0:1, at] if lo == 24 else jnp.zeros((1, 128), jnp.float32)
            weights = rim_weights(part, j, inside, above, below)
            w_wide[0, lo : lo + 8, at] = 1.0 - (4.0 * STEP) * weights[0]
            for i in (1, 2, 3, 4):
                w_wide[i, lo : lo + 8, at] = (4.0 * STEP) * weights[i]
    w_wide[:, 0:ROWS] = w_mid[:, 0:ROWS]

    b_buf[0] = widen(r_buf[0])
    b_buf[1] = apply(b_buf[0], w_wide) + widen(r_buf[1])
    b_buf[2] = apply(b_buf[1], w_wide) + widen(r_buf[2])
    u_buf[...] = apply(b_buf[2], w_wide) + widen(r_buf[3])
    u_rim = batch([
        downward(u_buf.at[16:24], cu.at[0:8]),
        upward(u_buf.at[24:32], cu.at[8:16]),
    ])
    b_rim = []
    for j in range(3):
        b_rim += batch([
            downward(b_buf.at[j, 16:24], cb.at[j, 0:8]),
            upward(b_buf.at[j, 24:32], cb.at[j, 8:16]),
        ])
    arrive(pg_halo)
    pg[0:1] = pg[0:1] + cpg[0]
    pg[15:16] = pg[15:16] + cpg[1]
    arrive(u_rim)
    u = u_buf[0:ROWS] + cu[...]
    y_buf[core] = u + pg[0:ROWS]

    y_swap = batch([remote(y_buf.at[core], y_buf.at[core], mate, s)])

    @pl.when(jnp.logical_and(core == 1, to_far))
    def _():
        far_src[...] = u
        far[0][0].start()

    arrive(y_swap)

    start = pl.multiple_of(core * (COLS - WIN), 128)
    window = pl.ds(start, WIN)
    yw[...] = apply(extend(y_buf[0, :, window], 24), w_mid, start) + extend(y_buf[1, :, window], 24)
    m1_copies = batch([
        remote(yw.at[0:ROWS], m1_in.at[0:ROWS], shift(2), s, to1, has1),
        remote(yw.at[16:17], m1_in.at[16:17], shift(2), s, to1, has1),
        remote(yw.at[23:24], m1_in.at[23:24], shift(2), s, to1, has1),
    ])

    z_rim = [
        downward(z_buf.at[16:24], cz.at[0:8]),
        upward(z_buf.at[24:32], cz.at[8:16]),
        upward(z_buf.at[0:3], hz.at[0:3]),
        downward(z_buf.at[13:16], hz.at[5:8]),
    ]
    batches.append(z_rim)

    def far_term(more):
        v = extend(far_in[...], 24)
        for _ in range(4):
            v = apply(v, w_mid)
        v = widen(v)
        for _ in range(more):
            v = apply(v, w_wide)
        return v

    @pl.when(core == 1)
    def _():
        arrive(far)
        z_buf[...] = extend(g_buf[...] + y_buf[0], 32) - far_term(3)
        begin(z_rim)


    arrive(m1_copies)
    m2[...] = apply(apply(m1_in[...], w_mid, start), w_mid, start) + yw[...]
    m2_copies = batch([
        remote(m2.at[0:ROWS], m2_in.at[0:ROWS], shift(4), s, to2, has2),
        remote(m2.at[16:19], m2_in.at[16:19], shift(4), s, to2, has2),
        remote(m2.at[21:24], m2_in.at[21:24], shift(4), s, to2, has2),
    ])

    arrive(b_rim)
    for j in range(3):
        base[j] = i_buf[j + 1] + (b_buf[j, 0:ROWS] + cb[j])

    @pl.when(core == 0)
    def _():
        arrive(far)
        z_buf[...] = extend(g_buf[...], 32) + far_term(2)
        begin(z_rim)

    arrive(m2_copies)
    wide = apply(apply(widen(m2_in[...]), w_wide, start), w_wide, start)
    wide = widen(m1_in[...]) + wide

    @pl.when(core == 0)
    def _():
        w_buf[0] = wide[:, 0:HALF]

    @pl.when(core == 1)
    def _():
        w_buf[1] = wide[:, WIN - HALF : WIN]

    mine = w_buf.at[core]
    w_rim = []
    for tm in (t, mate):
        w_rim += [
            downward(mine.at[16:21], cw.at[core, 0:5], tm),
            upward(mine.at[27:32], cw.at[core, 11:16], tm),
            upward(mine.at[0:4], hw.at[core, 0:4], tm),
            downward(mine.at[12:16], hw.at[core, 4:8], tm),
        ]
    w_rim = batch(w_rim)
    w_swap = batch([remote(mine, mine, mate, s)])

    near = lax.broadcasted_iota(jnp.int32, (8, COLS), 0) < 4

    def assemble(own, given, rim):
        return jnp.concatenate(
            [own[0:ROWS] + given, jnp.where(near, own[16:24], own[24:32]) + rim], axis=0
        )

    def halves(ref):
        return jnp.concatenate([ref[0], ref[1]], axis=1)

    arrive(z_rim)
    za[...] = assemble(z_buf[...], cz[...], hz[...])
    arrive(w_swap)
    arrive(w_rim)
    w = assemble(halves(w_buf), halves(cw), halves(hw))

    @pl.when(core == 0)
    def _():
        w_sum[...] = za[...] + w

    @pl.when(core == 1)
    def _():
        w_sum[...] = za[...] + apply(w, w_mid)

    state = w_sum[...]
    out[0] = i_buf[0] + state[0:ROWS]
    for j in (1, 2, 3):
        state = apply(state, w_mid)
        out[j] = base[j - 1] + state[0:ROWS]
    for copies in batches:
        each(copies, 1, lambda c: c.wait_send())


def per_device(forcing, iterate, permeability):
    def field(*shape):
        return pltpu.VMEM(shape, jnp.float32)

    scratch = [
        field(16, ROWS, COLS),
        field(4, ROWS, COLS),
        field(32, COLS),
        field(8, COLS),
        field(5, 24, COLS),
        field(5, 24, COLS),
        field(5, 32, COLS),
        field(2, 4, 24, COLS),
        field(4, 24, COLS),
        field(3, 32, COLS),
        field(ROWS, COLS),
        field(24, COLS),
        field(32, COLS),
        field(ROWS, COLS),
        field(3, ROWS, COLS),
        field(2, 1, COLS),
        field(ROWS, COLS),
        field(ROWS, COLS),
        field(2, ROWS, COLS),
        field(24, WIN),
        field(24, WIN),
        field(24, WIN),
        field(24, WIN),
        field(32, COLS),
        field(ROWS, COLS),
        field(8, COLS),
        field(24, COLS),
        field(2, 32, HALF),
        field(2, ROWS, HALF),
        field(2, 8, HALF),
        field(24, COLS),
        field(3, ROWS, COLS),
        pltpu.SemaphoreType.DMA((NCOPY,)),
        pltpu.SemaphoreType.DMA((NCOPY,)),
        pltpu.SemaphoreType.DMA((3,)),
    ]
    return pl.pallas_call(
        kernel,
        name="vcycle",
        out_shape=pltpu.VMEM(iterate.shape, iterate.dtype),
        in_specs=[pl.BlockSpec(memory_space=pltpu.HBM)] * 3,
        out_specs=pl.BlockSpec(memory_space=pltpu.VMEM),
        scratch_shapes=scratch,
        compiler_params=pltpu.CompilerParams(
            collective_id=0, has_side_effects=True, vmem_limit_bytes=24 * 2**20
        ),
    )(*(pltpu.with_memory_space_constraint(v, pltpu.HBM) for v in (forcing, iterate, permeability)))


def solution(mesh):
    in_specs = (P("tm", "space", None), P("tm", "space", None), P("space", None))
    out_specs = P("tm", "space", None)
    return jax.shard_map(
        per_device, mesh=mesh, in_specs=in_specs, out_specs=out_specs, check_vma=False
    )
```
